256 devices in a mesh: dp: 4 (over x), shard: 64 (over y, z, core).
Axes of the slice: x: 4, y: 4, z: 8, core: 2. Of those that a mesh axis runs over, the one named last changes fastest.
Arguments:
- grad_partial: bfloat16 [4, 16, 512, 14336], P('dp', None, 'shard'), may hold values from -6 to 6
- second_moment: float32 [16, 512, 14336], P(None, 'shard', 'dp'), may hold values from 0.002 to 3, as said below
- params: bfloat16 [16, 512, 14336], P(None, 'shard', 'dp'), may hold values from -6 to 6
- left_roots: bfloat16 [4, 64, 3, 512, 512], P('dp', 'shard'), may hold values from -1 to 4, as said below
- right_roots: bfloat16 [4, 64, 3, 512, 512], P('dp', 'shard'), may hold values from -1 to 4, as said below
- owners: int32 [4, 112, 1], replicated, may hold values from 0 to 63; in each aligned block of 112 rows (0 to 111, 112 to 223, ..., all dimensions but the last counted through in order) at most 3 rows name the same one
Outputs:
- updated: bfloat16 [16, 512, 14336], P(None, 'shard')
The draws below stay inside these ranges and needn't reach their ends.
Inputs may be any that keep to these rules, and one draw needn't show every extreme that they name: `second_moment`: second-moment estimates, positive. `left_roots`: symmetric factors. `right_roots`: symmetric factors. `owners`: in each group no owner is named by more than 3 blocks, a bound that some block reaches.
All inputs are finite; a program needn't handle non-finite values.
Results may differ from the reference program's by a relative error of at most 0.015.
Values may be sent and summed in bfloat16 or wider, within the bound.
A program may use at most 64 MiB of HBM per device.

```python
import math
import jax
import jax.numpy as jnp
import numpy as np
from jax import lax

FF = 14336
BS = 512
GROUPS = 4
BROWS = 16
BCOLS = 7
BLOCKS_GRP = 112
SLOTS = 3
N_DP = 4
N_SHARD = 64


def symmetric_factor(noise, diagonal):
    size = noise.shape[-1]
    eye = (jnp.arange(size)[:, None] == jnp.arange(size)[None, :]).astype(jnp.float32)
    mixed = (noise + jnp.swapaxes(noise, -1, -2)) * 0.7071
    return mixed * (1.0 - eye) + eye * diagonal[..., None]


def factor_draw(key):
    first, second = jax.random.split(key)
    shape = (GROUPS, N_SHARD, SLOTS, BS, BS)
    noise = jnp.clip(jax.random.normal(first, shape, jnp.float32), -5.0, 5.0) * (0.4 / BS ** 0.5)
    diagonal = jnp.exp(jax.random.uniform(second, shape[:-1], jnp.float32, 0.0, 1.09))
    return symmetric_factor(noise, diagonal).astype(jnp.bfloat16)


def draw_left_roots(key, part):
    key = jax.random.fold_in(key, 11)
    return factor_draw(key)


def draw_right_roots(key, part):
    key = jax.random.fold_in(key, 12)
    return factor_draw(key)


def draw_second_moment(key, part):
    key = jax.random.fold_in(key, 13)
    first = jax.random.fold_in(key, 0)
    third = jax.random.fold_in(key, 2)
    shape = (BROWS, BS, FF)
    rows = jnp.arange(BS, dtype=jnp.float32)[None, :, None]
    rising = 1.0 / (1.0 + 2.0 * rows / (BS - 1))
    coarse = jnp.exp(jax.random.uniform(third, (BROWS, 1, FF // BS, 1), jnp.float32, -2.3, 0.0))
    coarse = jnp.broadcast_to(coarse, (BROWS, 1, FF // BS, BS)).reshape(BROWS, 1, FF)
    base = jnp.exp(jax.random.uniform(first, shape, jnp.float32, -1.2, 1.09))
    return base * rising * coarse


def spiked(values, key, source, target, parts, factor):
    owner, partner = [(jnp.arange(values.shape[axis_at]) // (values.shape[axis_at] // parts)).reshape([-1 if axis == axis_at else 1 for axis in range(values.ndim)]) for axis_at in (source, target)]
    chosen = jax.random.permutation(key, parts)[partner]
    strong = (owner == chosen) | (owner == (partner + parts // 2) % parts)
    return jnp.where(strong, factor * values, values)


def levels(rng, dims, cuts, smallest, largest):
    def one(position, shards_of):
        draws = jax.random.uniform(jax.random.fold_in(jax.random.fold_in(rng, 6), position), (shards_of,), jnp.float32, smallest / len(cuts), largest / len(cuts))
        return jnp.repeat(jnp.exp(draws), dims[position] // shards_of).reshape((-1,) + (1,) * (len(dims) - position - 1))

    gain = one(*cuts[0])
    for cut in cuts[1:]:
        gain = gain * one(*cut)
    return gain


def assign_block(own_key, own, number, rows, amount, top, most, skew):
    order = jax.random.permutation(own_key, amount)
    heavy_load, ordinary = shares(amount, rows * top, most, skew, True), shares(amount, rows * top, most, skew, False)
    places = jnp.arange(amount)

    def named(tallies, turn):
        used = int((tallies > 0).sum())
        fixed = max(1, used // 4)
        passed = fixed + (places - fixed + turn * (used - fixed)) % max(1, amount - fixed)
        return jnp.zeros((amount,), jnp.int32).at[order[jnp.where(places < fixed, places, passed)]].set(jnp.asarray(tallies, jnp.int32))

    tallies = jnp.where(number % 4 == 0, named(heavy_load, number // 4), named(ordinary, number - number // 4 - 1))
    mixed = jax.random.permutation(jax.random.fold_in(own, 3), amount)
    donor, taker = mixed[0:amount // 2 * 2:2], mixed[1:amount // 2 * 2:2]
    margin = jnp.minimum(tallies[donor] - 1, most - tallies[taker]) // 2
    margin = jnp.where((donor == order[0]) | (taker == order[0]) | (tallies[taker] == 0), 0, jnp.maximum(margin, 0))
    passed = jax.random.randint(jax.random.fold_in(own, 4), (amount // 2,), 0, 1 << 20) % (margin + 1)
    tallies = tallies.at[donor].add(-passed).at[taker].add(passed)
    items = jnp.searchsorted(jnp.cumsum(tallies), jnp.arange(rows * top), side="right").astype(jnp.int32)
    grid = items.reshape(top, rows).T
    grid = grid[jax.random.permutation(jax.random.fold_in(own, 1), rows)]
    turn = jax.random.randint(jax.random.fold_in(own, 2), (rows, 1), 0, top)
    return jnp.take_along_axis(grid, (jnp.arange(top)[None, :] + turn) % top, axis=1)


def shares(number_of, total, reach, lean, full):
    loads = [(1 << 20) // math.isqrt(standing ** lean) + 1 for standing in range(1, number_of + 1)]
    largest = reach if full else min(reach, max(-(-total // number_of), total * loads[0] // sum(loads)))
    least = 1 if total - largest >= number_of - 1 else 0
    holding, spare = [largest] + [least] * (number_of - 1), total - largest - least * (number_of - 1)
    while spare > 0:
        candidates = [i for i in range(1, number_of) if holding[i] < largest] or [i for i in range(1, number_of) if holding[i] < reach]
        pool, remaining = sum([loads[i] for i in candidates]), spare
        for i in candidates:
            more = min(reach - holding[i], max(1, remaining * loads[i] // pool), spare)
            holding[i] = holding[i] + more
            spare = spare - more
    return np.array(holding)


def bell_draw(rng, dims, width, most, shards=(), held_as=jnp.bfloat16):
    factor_of = levels(rng, dims, shards, -0.22, 0.18) if shards else 1.0
    drawn = jax.random.normal(rng, dims, jnp.float32) * width * factor_of
    return jnp.minimum(jnp.maximum(drawn, -most), most).astype(held_as)


def heavy_noise(own_key, shape, spread, most, cuts, heavy, kind=jnp.bfloat16):
    drawn = spread * jax.random.normal(own_key, shape, jnp.float32)
    if cuts:
        drawn = drawn * levels(own_key, shape, cuts, -0.22, 0.18)
    return jnp.clip(spiked(drawn, jax.random.fold_in(own_key, 3), *heavy), -most, most).astype(kind)


def setup_inputs(seed: int = 0) -> dict:
    splits = jax.random.split(jax.random.key(seed), 7)
    grad_partial = heavy_noise(splits[0], (GROUPS, BROWS, BS, FF), 1.0, 6.0, ((0, 4), (2, 64)), (0, 3, 4, 2.0))
    second_moment = draw_second_moment(jax.random.fold_in(splits[6], 71), 0)
    params = bell_draw(splits[2], (BROWS, BS, FF), 1.0, 6.0, ((1, 64), (2, 4)))
    left_roots = draw_left_roots(jax.random.fold_in(splits[6], 71), 0)
    right_roots = draw_right_roots(jax.random.fold_in(splits[6], 71), 0)
    owners_keys = jax.random.split(jax.random.fold_in(splits[5], 1), GROUPS * BLOCKS_GRP // BLOCKS_GRP)
    owners_turns = jax.random.permutation(jax.random.fold_in(splits[5], 3), GROUPS * BLOCKS_GRP // BLOCKS_GRP)
    owners = jax.vmap(lambda own, number: assign_block(jax.random.fold_in(splits[5], 2), own, number, BLOCKS_GRP, N_SHARD, 1, SLOTS, 2))(owners_keys, owners_turns).reshape((GROUPS, BLOCKS_GRP, 1))
    return dict(grad_partial=grad_partial, second_moment=second_moment, params=params, left_roots=left_roots, right_roots=right_roots, owners=owners)


BETA2 = 0.95
EPS_ADAM = 1e-08
EPS_NORM = 1e-06
STEP_RATE = 0.5

def reference(grad_partial, second_moment, params, left_roots, right_roots, owners):
    grad = lax.optimization_barrier(jnp.sum(grad_partial.astype(jnp.float32), axis=0))
    vnew = BETA2 * second_moment + (1.0 - BETA2) * grad * grad
    adam = grad / (jnp.sqrt(vnew) + EPS_ADAM)
    gblocks = grad.astype(jnp.bfloat16).reshape(BROWS, BS, N_DP, BCOLS, BS)
    gblocks = gblocks.transpose(2, 0, 3, 1, 4).reshape(N_DP * BLOCKS_GRP, BS, BS)
    squares = lax.optimization_barrier(jnp.sum((adam * adam).reshape(BROWS, BS, N_DP, BCOLS, BS), axis=(1, 4)))
    adam_norm = jnp.sqrt(squares.transpose(1, 0, 2).reshape(N_DP * BLOCKS_GRP))
    table = owners[:, :, 0]
    hits = (table[:, :, None] == jnp.arange(N_SHARD, dtype=jnp.int32)[None, None, :]).astype(jnp.int32)
    rank = lax.optimization_barrier(jnp.sum((jnp.cumsum(hits, axis=1) - hits) * hits, axis=2)).astype(jnp.int32)
    groups = jnp.arange(N_DP, dtype=jnp.int32)[:, None]
    where = ((groups * N_SHARD + table) * SLOTS + rank).reshape(-1).astype(jnp.int32)
    lefts = left_roots.reshape(N_DP * N_SHARD * SLOTS, BS, BS)
    rights = right_roots.reshape(N_DP * N_SHARD * SLOTS, BS, BS)

    def one_block(item):
        block, spot, magnitude = item
        left = lefts[spot]
        right = rights[spot]
        half = jnp.dot(left, block, preferred_element_type=jnp.float32).astype(jnp.bfloat16)
        prec = jnp.dot(half, right, preferred_element_type=jnp.float32)
        pnorm = jnp.sqrt(jnp.sum(prec * prec))
        return (prec * (magnitude / (pnorm + EPS_NORM))).astype(jnp.bfloat16)
    steps = lax.map(one_block, (gblocks, where, adam_norm))
    steps = steps.reshape(N_DP, BROWS, BCOLS, BS, BS).transpose(1, 3, 0, 2, 4).reshape(BROWS, BS, FF)
    return (params.astype(jnp.float32) - STEP_RATE * steps.astype(jnp.float32)).astype(jnp.bfloat16)
```

```python
import functools
import jax
import jax.numpy as jnp
from jax import lax
from jax.experimental import pallas as pl
from jax.experimental.pallas import tpu as pltpu
from jax.sharding import PartitionSpec as P

BETA2 = 0.95
EPS_ADAM = 1e-08
EPS_NORM = 1e-06
STEP_RATE = 0.5
NY, NZ, NC = 4, 8, 2
LANES = 128
MESH = pl.DeviceIdType.MESH
F32, BF16 = jnp.float32, jnp.bfloat16


def wait_bytes(ref, sem):
    pltpu.make_async_copy(ref, ref, sem).wait()


def kernel(
    gp, sm, pr, lr, rr, ow, out,
    own, mid, far, comb, near, smv, prv, lv, rv, gf, acc,
    sel, selt, outgoing, incoming, half, prec, steps, returned, mine,
    nsrc, nz, nmid, npl,
    load_sem, rs_send, rs_recv, in_send, in_recv, ret_send, ret_recv,
    ag_send, ag_recv, n_send, n_recv,
):
    brows, bcols, pieces = own.shape[0], own.shape[1], own.shape[2]
    hb = brows // 2
    nb = brows * bcols
    shards, slots, rdev = outgoing.shape[1], outgoing.shape[2], outgoing.shape[3]
    bsize = lv.shape[1]
    d = lax.axis_index("dp")
    me = lax.axis_index("shard")
    y, z, c = me // (NZ * NC), (me // NC) % NZ, me % NC
    up, dn, op = (d + 1) % 4, (d + 3) % 4, (d + 2) % 4
    lo, hi = pl.ds(0, hb), pl.ds(hb, hb)

    def cols(group):
        return pl.ds(group * bcols, bcols)

    def peer(dy, dz, dc):
        return (((y + dy) % NY) * NZ + (z + dz) % NZ) * NC + (c + dc) % NC

    def for_peers(act):
        def outer(i, carry):
            plane = i // (NZ - 1)
            act(peer(plane // NC, 1 + i % (NZ - 1), plane % NC))
            return carry

        def inner(i, carry):
            act(peer(i // NC, 0, i % NC))
            return carry

        lax.fori_loop(0, (NZ - 1) * NY * NC, outer, 0)
        lax.fori_loop(1, NY * NC, inner, 0)

    barrier = pltpu.get_barrier_semaphore()
    for other in (up, dn):
        pl.semaphore_signal(barrier, 1, device_id=(other, me), device_id_type=MESH)
    for_peers(lambda t: pl.semaphore_signal(barrier, 1, device_id=(d, t), device_id_type=MESH))

    loads = [
        (gp.at[lo, cols(up)], mid.at[0]),
        (gp.at[hi, cols(dn)], mid.at[1]),
        (gp.at[:, cols(d)], own),
        (sm, smv),
        (lr, lv),
        (rr, rv),
        (pr, prv),
    ]
    loads = [pltpu.make_async_copy(a, b, load_sem.at[i]) for i, (a, b) in enumerate(loads)]
    for load in loads:
        load.start()

    table = ow[d].astype(F32)
    b0 = lax.broadcasted_iota(jnp.int32, (nb, nb), 0)
    b1 = lax.broadcasted_iota(jnp.int32, (nb, nb), 1)
    rows = jnp.broadcast_to(table, (nb, nb))
    column = jnp.sum(jnp.where(b0 == b1, rows, 0.0), axis=1, keepdims=True)
    same = jnp.where(rows == column, 1.0, 0.0)
    rank = jnp.sum(jnp.where(b0 < b1, same, 0.0), axis=0, keepdims=True)
    target = table * float(slots) + rank
    wide = nb * rdev
    e0 = lax.broadcasted_iota(jnp.int32, (nb, wide), 0) * rdev
    e1 = lax.broadcasted_iota(jnp.int32, (nb, wide), 1)
    spread = jnp.where((e1 >= e0) & (e1 < e0 + rdev), 1.0, 0.0).astype(BF16)
    wide_target = jnp.dot(
        jnp.broadcast_to(target, (8, nb)).astype(BF16), spread, preferred_element_type=F32
    )[0:1]
    l1 = lax.broadcasted_iota(jnp.int32, (1, wide), 1)
    wide_target = wide_target.astype(jnp.int32) * rdev + l1 % rdev
    t0 = lax.broadcasted_iota(jnp.int32, (wide, nb), 0)
    t1 = lax.broadcasted_iota(jnp.int32, (wide, nb), 1) * rdev
    tall = jnp.where((t0 >= t1) & (t0 < t1 + rdev), jnp.broadcast_to(target, (wide, nb)), 0.0)
    s0 = lax.broadcasted_iota(jnp.int32, (wide, 1), 0)
    tall_target = jnp.sum(tall, axis=1, keepdims=True).astype(jnp.int32) * rdev + s0 % rdev
    total_rows = shards * slots * rdev
    mrows = 8 * slots * rdev

    def fill(m, carry):
        r = lax.broadcasted_iota(jnp.int32, (mrows, wide), 0) + m * mrows
        sel[pl.ds(m * mrows, mrows), :] = jnp.where(r == wide_target, 1.0, 0.0).astype(BF16)
        return carry

    lax.fori_loop(0, total_rows // mrows, fill, 0)
    for m in range(total_rows // 512):
        r = lax.broadcasted_iota(jnp.int32, (wide, 512), 1) + m * 512
        selt[:, m * 512 : (m + 1) * 512] = jnp.where(r == tall_target, 1.0, 0.0).astype(BF16)

    pl.semaphore_wait(barrier, 2 + shards - 1)

    def rs(p, kind):
        src, dst, to = {
            "a": (gp.at[lo, cols(op), p], far.at[p, 0], up),
            "b": (gp.at[hi, cols(op), p], far.at[p, 1], dn),
            "c": (gp.at[hi, cols(up), p], near.at[p, 1], up),
            "d": (gp.at[lo, cols(dn), p], near.at[p, 2], dn),
            "e": (comb.at[p, 0], near.at[p, 0], up),
            "f": (comb.at[p, 1], near.at[p, 3], dn),
        }[kind]
        n = "abcdef".index(kind)
        return pltpu.make_async_remote_copy(
            src, dst, rs_send.at[p, n], rs_recv.at[p, n], device_id=(to, me), device_id_type=MESH
        )

    def start(p, kinds):
        if p < pieces:
            for kind in kinds:
                rs(p, kind).start()

    def combine(p):
        for h, kind in enumerate("ab"):
            rs(p, kind).wait_recv()

            def add(r, carry, h=h):
                s = mid[h, r, :, p].astype(F32) + far[p, h, r].astype(F32)
                comb[p, h, r] = s.astype(BF16)
                return carry

            lax.fori_loop(0, hb, add, 0)
            rs(p, "ef"[h]).start()

    def exchange(src, dst, p, send, recv):
        def act(t):
            pltpu.make_async_remote_copy(
                src.at[p, t], dst.at[p, me], send.at[p], recv.at[p], device_id=(d, t), device_id_type=MESH
            ).start()

        for_peers(act)
        pltpu.make_async_copy(src.at[p, me], dst.at[p, me], recv.at[p]).start()

    def finish(p):
        for kind in "cdef":
            rs(p, kind).wait_recv()
        for h in range(2):

            def one(r, carry, h=h):
                b = h * hb + r
                g = own[b, :, p].astype(F32) + near[p, h, r].astype(F32) + near[p, 2 + h, r].astype(F32)
                vnew = BETA2 * smv[b, :, p] + (1.0 - BETA2) * g * g
                adam = g / (jnp.sqrt(vnew) + EPS_ADAM)
                gf[b] = g
                acc[b] = adam * adam if p == 0 else acc[b] + adam * adam
                return carry

            lax.fori_loop(0, hb, one, 0)
        blocks = gf[...].reshape(wide, LANES).astype(BF16)

        def pick(m, carry):
            got = jnp.dot(sel[pl.ds(m * mrows, mrows), :], blocks, preferred_element_type=F32)
            outgoing[p, pl.ds(m * 8, 8)] = got.reshape(8, slots, rdev, LANES).astype(BF16)
            return carry

        lax.fori_loop(0, shards // 8, pick, 0)
        exchange(outgoing, incoming, p, in_send, in_recv)

    start(0, "abcd")
    start(1, "ab")
    for load in loads[:4]:
        load.wait()
    for p in range(pieces + 1):
        if p < pieces:
            combine(p)
            start(p + 1, "cd")
            start(p + 2, "ab")
        if p > 0:
            finish(p - 1)

    sums = jnp.sum(jnp.sum(acc[...].reshape(nb, rdev, LANES), axis=1), axis=1, keepdims=True)
    n0 = lax.broadcasted_iota(jnp.int32, (nb, LANES), 0)
    n1 = lax.broadcasted_iota(jnp.int32, (nb, LANES), 1)
    spots = jnp.where(n0 == n1, jnp.broadcast_to(sums, (nb, LANES)), 0.0)
    nsrc[...] = jnp.sum(spots.reshape(nb // 8, 8, LANES), axis=0)
    for i in range(1, NZ):
        pltpu.make_async_remote_copy(
            nsrc, nz.at[z], n_send.at[0], n_recv.at[0], device_id=(d, peer(0, i, 0)), device_id_type=MESH
        ).start()
    pltpu.make_async_copy(nsrc, nz.at[z], n_recv.at[0]).start()

    for load in loads[4:]:
        load.wait()

    def multiply(p):
        wait_bytes(incoming.at[p], in_recv.at[p])
        for k in range(slots):
            g = incoming[p, :, k].astype(F32).reshape(bsize, LANES).astype(BF16)
            half[k, :, p * LANES : (p + 1) * LANES] = jnp.dot(
                lv[k], g, preferred_element_type=F32
            ).astype(BF16)

    for p in range(pieces - 1):
        multiply(p)
    cut = (pieces - 1) * LANES
    for k in range(slots):
        prec[k] = jnp.dot(half[k, :, :cut], rv[k, :cut, :], preferred_element_type=F32)

    wait_bytes(nz, n_recv.at[0])
    nmid[...] = jnp.sum(nz[...], axis=0)
    for i in range(1, NY * NC):
        pltpu.make_async_remote_copy(
            nmid, npl.at[y * NC + c], n_send.at[1], n_recv.at[1],
            device_id=(d, peer(i // NC, 0, i % NC)), device_id_type=MESH,
        ).start()
    pltpu.make_async_copy(nmid, npl.at[y * NC + c], n_recv.at[1]).start()

    multiply(pieces - 1)
    for k in range(slots):
        prec[k] += jnp.dot(half[k, :, cut:], rv[k, cut:, :], preferred_element_type=F32)

    wait_bytes(npl, n_recv.at[1])
    totals = jnp.sum(jnp.sum(npl[...], axis=0), axis=0, keepdims=True)[:, :nb]
    scales = []
    for k in range(slots):
        here = (me * slots + k).astype(F32)
        adam_sq = jnp.sum(jnp.where(target == here, totals, 0.0), axis=1, keepdims=True)
        x = prec[k]
        pnorm = jnp.sqrt(jnp.sum(jnp.sum(x * x, axis=0, keepdims=True), axis=1, keepdims=True))
        scales.append(jnp.sqrt(adam_sq) / (pnorm + EPS_NORM))

    for p in range(pieces):
        for k in range(slots):
            x = prec[k, :, p * LANES : (p + 1) * LANES] * scales[k]
            steps[p, :, k] = x.reshape(shards, rdev, LANES).astype(BF16)
        exchange(steps, returned, p, ret_send, ret_recv)

    def ag(p, n):
        src, rows, group, to = [
            (mine, lo, d, up),
            (mine, hi, d, dn),
            (mine, hi, d, up),
            (mine, lo, d, dn),
            (out, lo, dn, up),
            (out, hi, up, dn),
        ][n]
        dst = out.at[rows, cols(group), p]
        src = mine.at[p, rows] if src is mine else dst
        return pltpu.make_async_remote_copy(
            src, dst, ag_send.at[p, n], ag_recv.at[p, n], device_id=(to, me), device_id_type=MESH
        )

    def ag_arrived(p, n):
        rows, group = [(lo, dn), (hi, up), (hi, dn), (lo, up), (lo, op), (hi, op)][n]
        wait_bytes(out.at[rows, cols(group), p], ag_recv.at[p, n])

    keep = [
        pltpu.make_async_copy(mine.at[p], out.at[:, cols(d), p], load_sem.at[p]) for p in range(pieces)
    ]

    def forward(p):
        for n in (0, 1):
            ag_arrived(p, n)
            ag(p, 4 + n).start()

    for p in range(pieces):
        wait_bytes(returned.at[p], ret_recv.at[p])
        back = returned[p].astype(F32).reshape(total_rows, LANES).astype(BF16)
        placed = jnp.dot(selt[...], back, preferred_element_type=F32)
        placed = placed.reshape(brows, bcols, rdev, LANES)
        mine[p] = (prv[:, :, p].astype(F32) - STEP_RATE * placed).astype(BF16)
        for n in range(4):
            ag(p, n).start()
        keep[p].start()
        if p > 0:
            forward(p - 1)
    forward(pieces - 1)

    for p in range(pieces):
        for n in range(2, 6):
            ag_arrived(p, n)
        keep[p].wait()
        for n in range(6):
            ag(p, n).wait_send()
        for kind in "abcdef":
            rs(p, kind).wait_send()
        wait_bytes(outgoing.at[p, pl.ds(0, shards - 1)], in_send.at[p])
        wait_bytes(steps.at[p, pl.ds(0, shards - 1)], ret_send.at[p])
    wait_bytes(nz.at[pl.ds(0, NZ - 1)], n_send.at[0])
    wait_bytes(npl.at[pl.ds(0, NY * NC - 1)], n_send.at[1])


def body(grad_partial, second_moment, params, left_roots, right_roots, owners):
    shards = lax.axis_size("shard")
    brows, rdev, ffall = grad_partial.shape[1:]
    slots, bsize = left_roots.shape[2], left_roots.shape[3]
    ffgroup = second_moment.shape[2]
    bcols = ffgroup // bsize
    groups = ffall // ffgroup
    pieces = bsize // LANES
    hb = brows // 2
    wide = brows * bcols * rdev

    def tiles(x):
        n = x.shape[-1]
        x = x.reshape(brows, rdev, n // LANES, LANES).transpose(0, 2, 1, 3)
        return x.reshape(brows, n // bsize, pieces, rdev, LANES)

    hbm = pl.BlockSpec(memory_space=pl.ANY)
    vmem = pl.BlockSpec(memory_space=pltpu.VMEM)
    dma = pltpu.SemaphoreType.DMA
    tile = (rdev, LANES)
    out = pl.pallas_call(
        kernel,
        out_shape=jax.ShapeDtypeStruct((brows, groups * bcols, pieces) + tile, BF16),
        in_specs=[hbm] * 5 + [vmem],
        out_specs=hbm,
        scratch_shapes=[
            pltpu.VMEM((brows, bcols, pieces) + tile, BF16),
            pltpu.VMEM((2, hb, bcols, pieces) + tile, BF16),
            pltpu.VMEM((pieces, 2, hb, bcols) + tile, BF16),
            pltpu.VMEM((pieces, 2, hb, bcols) + tile, BF16),
            pltpu.VMEM((pieces, 4, hb, bcols) + tile, BF16),
            pltpu.VMEM((brows, bcols, pieces) + tile, F32),
            pltpu.VMEM((brows, bcols, pieces) + tile, BF16),
            pltpu.VMEM((slots, bsize, bsize), BF16),
            pltpu.VMEM((slots, bsize, bsize), BF16),
            pltpu.VMEM((brows, bcols) + tile, F32),
            pltpu.VMEM((brows, bcols) + tile, F32),
            pltpu.VMEM((shards * slots * rdev, wide), BF16),
            pltpu.VMEM((wide, shards * slots * rdev), BF16),
            pltpu.VMEM((pieces, shards, slots) + tile, BF16),
            pltpu.VMEM((pieces, shards, slots) + tile, BF16),
            pltpu.VMEM((slots, bsize, bsize), BF16),
            pltpu.VMEM((slots, bsize, bsize), F32),
            pltpu.VMEM((pieces, shards, slots) + tile, BF16),
            pltpu.VMEM((pieces, shards, slots) + tile, BF16),
            pltpu.VMEM((pieces, brows, bcols) + tile, BF16),
            pltpu.VMEM((8, LANES), F32),
            pltpu.VMEM((NZ, 8, LANES), F32),
            pltpu.VMEM((8, LANES), F32),
            pltpu.VMEM((NY * NC, 8, LANES), F32),
            dma((7,)),
            dma((pieces, 6)),
            dma((pieces, 6)),
            dma((pieces,)),
            dma((pieces,)),
            dma((pieces,)),
            dma((pieces,)),
            dma((pieces, 6)),
            dma((pieces, 6)),
            dma((2,)),
            dma((2,)),
        ],
        compiler_params=pltpu.CompilerParams(
            collective_id=0, has_side_effects=True, vmem_limit_bytes=50 * 2**20
        ),
    )(
        tiles(grad_partial[0]),
        tiles(second_moment),
        tiles(params),
        left_roots[0, 0],
        right_roots[0, 0],
        owners.transpose(0, 2, 1),
    )
    out = out.reshape(brows, ffall // LANES, rdev, LANES).transpose(0, 2, 1, 3)
    return out.reshape(brows, rdev, ffall)


def solution(mesh):
    return jax.shard_map(
        body,
        mesh=mesh,
        in_specs=(
            P("dp", None, "shard", None),
            P(None, "shard", "dp"),
            P(None, "shard", "dp"),
            P("dp", "shard", None, None, None),
            P("dp", "shard", None, None, None),
            P(),
        ),
        out_specs=P(None, "shard", None),
        check_vma=False,
    )
```

```python
import functools
import jax
import jax.numpy as jnp
from jax import lax
from jax.experimental import pallas as pl
from jax.experimental.pallas import tpu as pltpu
from jax.sharding import PartitionSpec as P

BETA2 = 0.95
EPS_ADAM = 1e-08
EPS_NORM = 1e-06
STEP_RATE = 0.5
NY, NZ, NC = 4, 8, 2
LANES = 128
MESH = pl.DeviceIdType.MESH
F32, BF16 = jnp.float32, jnp.bfloat16


def wait_bytes(ref, sem):
    pltpu.make_async_copy(ref, ref, sem).wait()


def kernel(
    gp, sm, pr, lr, rr, ow, out,
    own, mid, far, comb, near, smv, prv, lv, rv, gf, acc,
    sel, selt, outgoing, incoming, half, prec, steps, returned, mine,
    nsrc, nz, nmid, npl,
    load_sem, rs_send, rs_recv, in_send, in_recv, ret_send, ret_recv,
    ag_send, ag_recv, n_send, n_recv, met,
):
    brows, bcols, pieces = own.shape[0], own.shape[1], own.shape[2]
    hb = brows // 2
    nb = brows * bcols
    shards, slots, rdev = outgoing.shape[1], outgoing.shape[2], outgoing.shape[3]
    bsize = lv.shape[1]
    d = lax.axis_index("dp")
    me = lax.axis_index("shard")
    y, z, c = me // (NZ * NC), (me // NC) % NZ, me % NC
    up, dn, op = (d + 1) % 4, (d + 3) % 4, (d + 2) % 4
    lo, hi = pl.ds(0, hb), pl.ds(hb, hb)

    def cols(group):
        return pl.ds(group * bcols, bcols)

    def peer(dy, dz, dc):
        return (((y + dy) % NY) * NZ + (z + dz) % NZ) * NC + (c + dc) % NC

    def for_peers(act):
        def outer(i, carry):
            plane = i // (NZ - 1)
            act(peer(plane // NC, 1 + i % (NZ - 1), plane % NC))
            return carry

        def inner(i, carry):
            act(peer(i // NC, 0, i % NC))
            return carry

        lax.fori_loop(0, (NZ - 1) * NY * NC, outer, 0)
        lax.fori_loop(1, NY * NC, inner, 0)

    bits = (shards - 1).bit_length()
    flips = [me + (1 - 2 * ((me // 2**k) % 2)) * 2**k for k in range(bits)]
    barrier = pltpu.get_barrier_semaphore()
    for other in (up, dn):
        pl.semaphore_signal(barrier, 1, device_id=(other, me), device_id_type=MESH)
    for other in flips:
        pl.semaphore_signal(barrier, 1, device_id=(d, other), device_id_type=MESH)

    def spread_barrier(rounds):
        for k in rounds:
            pl.semaphore_signal(met.at[k], 1, device_id=(d, flips[k]), device_id_type=MESH)
            pl.semaphore_wait(met.at[k], 1)

    loads = [
        (gp.at[lo, cols(up)], mid.at[0]),
        (gp.at[hi, cols(dn)], mid.at[1]),
        (gp.at[:, cols(d)], own),
        (sm, smv),
        (lr, lv),
        (rr, rv),
        (pr, prv),
    ]
    loads = [pltpu.make_async_copy(a, b, load_sem.at[i]) for i, (a, b) in enumerate(loads)]
    for load in loads:
        load.start()

    pl.semaphore_wait(barrier, 2 + bits)

    def rs(p, kind):
        src, dst, to = {
            "a": (gp.at[lo, cols(op), p], far.at[p, 0], up),
            "b": (gp.at[hi, cols(op), p], far.at[p, 1], dn),
            "c": (gp.at[hi, cols(up), p], near.at[p, 1], up),
            "d": (gp.at[lo, cols(dn), p], near.at[p, 2], dn),
            "e": (comb.at[p, 0], near.at[p, 0], up),
            "f": (comb.at[p, 1], near.at[p, 3], dn),
        }[kind]
        n = "abcdef".index(kind)
        return pltpu.make_async_remote_copy(
            src, dst, rs_send.at[p, n], rs_recv.at[p, n], device_id=(to, me), device_id_type=MESH
        )

    def start(p, kinds):
        if p < pieces:
            for kind in kinds:
                rs(p, kind).start()

    def combine(p):
        for h, kind in enumerate("ab"):
            rs(p, kind).wait_recv()

            def add(r, carry, h=h):
                s = mid[h, r, :, p].astype(F32) + far[p, h, r].astype(F32)
                comb[p, h, r] = s.astype(BF16)
                return carry

            lax.fori_loop(0, hb, add, 0)
            rs(p, "ef"[h]).start()

    def exchange(src, dst, p, send, recv):
        def act(t):
            pltpu.make_async_remote_copy(
                src.at[p, t], dst.at[p, me], send.at[p], recv.at[p], device_id=(d, t), device_id_type=MESH
            ).start()

        for_peers(act)
        pltpu.make_async_copy(src.at[p, me], dst.at[p, me], recv.at[p]).start()

    def finish(p):
        for kind in "cdef":
            rs(p, kind).wait_recv()
        for h in range(2):

            def one(r, carry, h=h):
                b = h * hb + r
                g = own[b, :, p].astype(F32) + near[p, h, r].astype(F32)
                gf[b] = g + near[p, 2 + h, r].astype(F32)
                return carry

            lax.fori_loop(0, hb, one, 0)
        blocks = gf[...].reshape(wide, LANES).astype(BF16)

        def pick(m, carry):
            got = jnp.dot(sel[pl.ds(m * mrows, mrows), :], blocks, preferred_element_type=F32)
            outgoing[p, pl.ds(m * 8, 8)] = got.reshape(8, slots, rdev, LANES).astype(BF16)
            return carry

        lax.fori_loop(0, shards // 8, pick, 0)
        exchange(outgoing, incoming, p, in_send, in_recv)

        def norms(b, carry):
            g = gf[b]
            vnew = BETA2 * smv[b, :, p] + (1.0 - BETA2) * g * g
            adam = g / (jnp.sqrt(vnew) + EPS_ADAM)
            acc[b] = adam * adam if p == 0 else acc[b] + adam * adam
            return carry

        lax.fori_loop(0, brows, norms, 0)

    start(0, "abcd")
    start(1, "ab")
    spread_barrier(range(0, bits // 2))
    table = ow[d].astype(F32)
    b0 = lax.broadcasted_iota(jnp.int32, (nb, nb), 0)
    b1 = lax.broadcasted_iota(jnp.int32, (nb, nb), 1)
    rows = jnp.broadcast_to(table, (nb, nb))
    column = jnp.sum(jnp.where(b0 == b1, rows, 0.0), axis=1, keepdims=True)
    same = jnp.where(rows == column, 1.0, 0.0)
    rank = jnp.sum(jnp.where(b0 < b1, same, 0.0), axis=0, keepdims=True)
    target = table * float(slots) + rank
    wide = nb * rdev
    e0 = lax.broadcasted_iota(jnp.int32, (nb, wide), 0) * rdev
    e1 = lax.broadcasted_iota(jnp.int32, (nb, wide), 1)
    spread = jnp.where((e1 >= e0) & (e1 < e0 + rdev), 1.0, 0.0).astype(BF16)
    wide_target = jnp.dot(
        jnp.broadcast_to(target, (8, nb)).astype(BF16), spread, preferred_element_type=F32
    )[0:1]
    l1 = lax.broadcasted_iota(jnp.int32, (1, wide), 1)
    wide_target = wide_target.astype(jnp.int32) * rdev + l1 % rdev
    t0 = lax.broadcasted_iota(jnp.int32, (wide, nb), 0)
    t1 = lax.broadcasted_iota(jnp.int32, (wide, nb), 1) * rdev
    tall = jnp.where((t0 >= t1) & (t0 < t1 + rdev), jnp.broadcast_to(target, (wide, nb)), 0.0)
    s0 = lax.broadcasted_iota(jnp.int32, (wide, 1), 0)
    tall_target = jnp.sum(tall, axis=1, keepdims=True).astype(jnp.int32) * rdev + s0 % rdev
    total_rows = shards * slots * rdev
    mrows = 8 * slots * rdev

    def fill(m, carry):
        r = lax.broadcasted_iota(jnp.int32, (mrows, wide), 0) + m * mrows
        sel[pl.ds(m * mrows, mrows), :] = jnp.where(r == wide_target, 1.0, 0.0).astype(BF16)
        return carry

    lax.fori_loop(0, total_rows // mrows, fill, 0)

    for load in loads[:2]:
        load.wait()
    for p in range(pieces + 1):
        if p < pieces:
            combine(p)
            start(p + 1, "cd")
            start(p + 2, "ab")
        if p == 0:
            spread_barrier(range(bits // 2, bits))
            for load in loads[2:4]:
                load.wait()
        if p > 0:
            finish(p - 1)

    sums = jnp.sum(jnp.sum(acc[...].reshape(nb, rdev, LANES), axis=1), axis=1, keepdims=True)
    n0 = lax.broadcasted_iota(jnp.int32, (nb, LANES), 0)
    n1 = lax.broadcasted_iota(jnp.int32, (nb, LANES), 1)
    spots = jnp.where(n0 == n1, jnp.broadcast_to(sums, (nb, LANES)), 0.0)
    nsrc[...] = jnp.sum(spots.reshape(nb // 8, 8, LANES), axis=0)
    for i in range(1, NZ):
        pltpu.make_async_remote_copy(
            nsrc, nz.at[z], n_send.at[0], n_recv.at[0], device_id=(d, peer(0, i, 0)), device_id_type=MESH
        ).start()
    pltpu.make_async_copy(nsrc, nz.at[z], n_recv.at[0]).start()

    for m in range(total_rows // 512):
        r = lax.broadcasted_iota(jnp.int32, (wide, 512), 1) + m * 512
        selt[:, m * 512 : (m + 1) * 512] = jnp.where(r == tall_target, 1.0, 0.0).astype(BF16)

    for load in loads[4:]:
        load.wait()

    def multiply(p):
        wait_bytes(incoming.at[p], in_recv.at[p])
        for k in range(slots):
            g = incoming[p, :, k].astype(F32).reshape(bsize, LANES).astype(BF16)
            half[k, :, p * LANES : (p + 1) * LANES] = jnp.dot(
                lv[k], g, preferred_element_type=F32
            ).astype(BF16)

    for p in range(pieces - 1):
        multiply(p)
    cut = (pieces - 1) * LANES
    for k in range(slots):
        prec[k] = jnp.dot(half[k, :, :cut], rv[k, :cut, :], preferred_element_type=F32)

    wait_bytes(nz, n_recv.at[0])
    nmid[...] = jnp.sum(nz[...], axis=0)
    for i in range(1, NY * NC):
        pltpu.make_async_remote_copy(
            nmid, npl.at[y * NC + c], n_send.at[1], n_recv.at[1],
            device_id=(d, peer(i // NC, 0, i % NC)), device_id_type=MESH,
        ).start()
    pltpu.make_async_copy(nmid, npl.at[y * NC + c], n_recv.at[1]).start()

    multiply(pieces - 1)
    squares = []
    for k in range(slots):
        total = jnp.zeros((1, bsize), F32)
        for r in range(0, bsize, LANES):
            x = prec[k, r : r + LANES] + jnp.dot(
                half[k, r : r + LANES, cut:], rv[k, cut:, :], preferred_element_type=F32
            )
            prec[k, r : r + LANES] = x
            total += jnp.sum(x * x, axis=0, keepdims=True)
        squares.append(jnp.sum(total, axis=1, keepdims=True))

    wait_bytes(npl, n_recv.at[1])
    totals = jnp.sum(jnp.sum(npl[...], axis=0), axis=0, keepdims=True)[:, :nb]
    scales = []
    for k in range(slots):
        here = (me * slots + k).astype(F32)
        adam_sq = jnp.sum(jnp.where(target == here, totals, 0.0), axis=1, keepdims=True)
        scales.append(jnp.sqrt(adam_sq) / (jnp.sqrt(squares[k]) + EPS_NORM))

    for p in range(pieces):
        for k in range(slots):
            x = prec[k, :, p * LANES : (p + 1) * LANES] * scales[k]
            steps[p, :, k] = x.reshape(shards, rdev, LANES).astype(BF16)
        exchange(steps, returned, p, ret_send, ret_recv)

    def ag(p, n):
        src, rows, group, to = [
            (mine, lo, d, up),
            (mine, hi, d, dn),
            (mine, hi, d, up),
            (mine, lo, d, dn),
            (out, lo, dn, up),
            (out, hi, up, dn),
        ][n]
        dst = out.at[rows, cols(group), p]
        src = mine.at[p, rows] if src is mine else dst
        return pltpu.make_async_remote_copy(
            src, dst, ag_send.at[p, n], ag_recv.at[p, n], device_id=(to, me), device_id_type=MESH
        )

    def ag_arrived(p, n):
        rows, group = [(lo, dn), (hi, up), (hi, dn), (lo, up), (lo, op), (hi, op)][n]
        wait_bytes(out.at[rows, cols(group), p], ag_recv.at[p, n])

    keep = [
        pltpu.make_async_copy(mine.at[p], out.at[:, cols(d), p], load_sem.at[p]) for p in range(pieces)
    ]

    def forward(p):
        for n in (0, 1):
            ag_arrived(p, n)
            ag(p, 4 + n).start()

    for p in range(pieces):
        wait_bytes(returned.at[p], ret_recv.at[p])
        back = returned[p].astype(F32).reshape(total_rows, LANES).astype(BF16)
        placed = jnp.dot(selt[...], back, preferred_element_type=F32)
        placed = placed.reshape(brows, bcols, rdev, LANES)
        mine[p] = (prv[:, :, p].astype(F32) - STEP_RATE * placed).astype(BF16)
        for n in range(4):
            ag(p, n).start()
        keep[p].start()
        if p > 0:
            forward(p - 1)
    forward(pieces - 1)

    for p in range(pieces):
        for n in range(2, 6):
            ag_arrived(p, n)
        keep[p].wait()
        for n in range(6):
            ag(p, n).wait_send()
        for kind in "abcdef":
            rs(p, kind).wait_send()
        wait_bytes(outgoing.at[p, pl.ds(0, shards - 1)], in_send.at[p])
        wait_bytes(steps.at[p, pl.ds(0, shards - 1)], ret_send.at[p])
    wait_bytes(nz.at[pl.ds(0, NZ - 1)], n_send.at[0])
    wait_bytes(npl.at[pl.ds(0, NY * NC - 1)], n_send.at[1])


def body(grad_partial, second_moment, params, left_roots, right_roots, owners):
    shards = lax.axis_size("shard")
    brows, rdev, ffall = grad_partial.shape[1:]
    slots, bsize = left_roots.shape[2], left_roots.shape[3]
    ffgroup = second_moment.shape[2]
    bcols = ffgroup // bsize
    groups = ffall // ffgroup
    pieces = bsize // LANES
    hb = brows // 2
    wide = brows * bcols * rdev

    def tiles(x):
        n = x.shape[-1]
        x = x.reshape(brows, rdev, n // LANES, LANES).transpose(0, 2, 1, 3)
        return x.reshape(brows, n // bsize, pieces, rdev, LANES)

    hbm = pl.BlockSpec(memory_space=pl.ANY)
    vmem = pl.BlockSpec(memory_space=pltpu.VMEM)
    dma = pltpu.SemaphoreType.DMA
    tile = (rdev, LANES)
    out = pl.pallas_call(
        kernel,
        out_shape=jax.ShapeDtypeStruct((brows, groups * bcols, pieces) + tile, BF16),
        in_specs=[hbm] * 5 + [vmem],
        out_specs=hbm,
        scratch_shapes=[
            pltpu.VMEM((brows, bcols, pieces) + tile, BF16),
            pltpu.VMEM((2, hb, bcols, pieces) + tile, BF16),
            pltpu.VMEM((pieces, 2, hb, bcols) + tile, BF16),
            pltpu.VMEM((pieces, 2, hb, bcols) + tile, BF16),
            pltpu.VMEM((pieces, 4, hb, bcols) + tile, BF16),
            pltpu.VMEM((brows, bcols, pieces) + tile, F32),
            pltpu.VMEM((brows, bcols, pieces) + tile, BF16),
            pltpu.VMEM((slots, bsize, bsize), BF16),
            pltpu.VMEM((slots, bsize, bsize), BF16),
            pltpu.VMEM((brows, bcols) + tile, F32),
            pltpu.VMEM((brows, bcols) + tile, F32),
            pltpu.VMEM((shards * slots * rdev, wide), BF16),
            pltpu.VMEM((wide, shards * slots * rdev), BF16),
            pltpu.VMEM((pieces, shards, slots) + tile, BF16),
            pltpu.VMEM((pieces, shards, slots) + tile, BF16),
            pltpu.VMEM((slots, bsize, bsize), BF16),
            pltpu.VMEM((slots, bsize, bsize), F32),
            pltpu.VMEM((pieces, shards, slots) + tile, BF16),
            pltpu.VMEM((pieces, shards, slots) + tile, BF16),
            pltpu.VMEM((pieces, brows, bcols) + tile, BF16),
            pltpu.VMEM((8, LANES), F32),
            pltpu.VMEM((NZ, 8, LANES), F32),
            pltpu.VMEM((8, LANES), F32),
            pltpu.VMEM((NY * NC, 8, LANES), F32),
            dma((7,)),
            dma((pieces, 6)),
            dma((pieces, 6)),
            dma((pieces,)),
            dma((pieces,)),
            dma((pieces,)),
            dma((pieces,)),
            dma((pieces, 6)),
            dma((pieces, 6)),
            dma((2,)),
            dma((2,)),
            pltpu.SemaphoreType.REGULAR(((shards - 1).bit_length(),)),
        ],
        compiler_params=pltpu.CompilerParams(
            collective_id=0, has_side_effects=True, vmem_limit_bytes=60 * 2**20
        ),
    )(
        tiles(grad_partial[0]),
        tiles(second_moment),
        tiles(params),
        left_roots[0, 0],
        right_roots[0, 0],
        owners.transpose(0, 2, 1),
    )
    out = out.reshape(brows, ffall // LANES, rdev, LANES).transpose(0, 2, 1, 3)
    return out.reshape(brows, rdev, ffall)


def solution(mesh):
    return jax.shard_map(
        body,
        mesh=mesh,
        in_specs=(
            P("dp", None, "shard", None),
            P(None, "shard", "dp"),
            P(None, "shard", "dp"),
            P("dp", "shard", None, None, None),
            P("dp", "shard", None, None, None),
            P(),
        ),
        out_specs=P(None, "shard", None),
        check_vma=False,
    )
```

```python
import functools
import jax
import jax.numpy as jnp
from jax import lax
from jax.experimental import pallas as pl
from jax.experimental.pallas import tpu as pltpu
from jax.sharding import PartitionSpec as P

BETA2 = 0.95
EPS_ADAM = 1e-08
EPS_NORM = 1e-06
STEP_RATE = 0.5
NY, NZ, NC = 4, 8, 2
LANES = 128
MESH = pl.DeviceIdType.MESH
F32, BF16 = jnp.float32, jnp.bfloat16


def wait_bytes(ref, sem):
    pltpu.make_async_copy(ref, ref, sem).wait()


def kernel(
    gp, sm, pr, lr, rr, ow, out,
    own, mid, far, comb, near, smv, prv, lv, rv, gf, acc,
    sel, selt, outgoing, incoming, half, prec, steps, returned, mine,
    nsrc, nz, nmid, npl,
    load_sem, rs_send, rs_recv, in_send, in_recv, ret_send, ret_recv,
    ag_send, ag_recv, n_send, n_recv, met,
):
    brows, bcols, pieces = own.shape[0], own.shape[1], own.shape[2]
    hb = brows // 2
    nb = brows * bcols
    shards, slots, rdev = outgoing.shape[1], outgoing.shape[2], outgoing.shape[3]
    bsize = lv.shape[1]
    d = lax.axis_index("dp")
    me = lax.axis_index("shard")
    y, z, c = me // (NZ * NC), (me // NC) % NZ, me % NC
    up, dn, op = (d + 1) % 4, (d + 3) % 4, (d + 2) % 4
    lo, hi = pl.ds(0, hb), pl.ds(hb, hb)
    last = pieces - 1

    def cols(group):
        return pl.ds(group * bcols, bcols)

    def peer(dy, dz, dc):
        return (((y + dy) % NY) * NZ + (z + dz) % NZ) * NC + (c + dc) % NC

    def for_peers(act):
        def outer(i, carry):
            plane = i // (NZ - 1)
            act(peer(plane // NC, 1 + i % (NZ - 1), plane % NC))
            return carry

        def inner(i, carry):
            act(peer(i // NC, 0, i % NC))
            return carry

        lax.fori_loop(0, (NZ - 1) * NY * NC, outer, 0)
        lax.fori_loop(1, NY * NC, inner, 0)

    zh = NZ // 4
    digits = [
        [peer(i, 0, 0) for i in range(1, NY)],
        [(y * NZ + z // 4 * 4 + (z + i) % 4) * NC + c for i in range(1, 4)],
        [
            (y * NZ + (z // 4 + i // NC) % zh * 4 + z % 4) * NC + (c + i % NC) % NC
            for i in range(1, zh * NC)
        ],
    ]
    barrier = pltpu.get_barrier_semaphore()
    for other in (up, dn):
        pl.semaphore_signal(barrier, 1, device_id=(other, me), device_id_type=MESH)
    for other in sum(digits, []):
        pl.semaphore_signal(barrier, 1, device_id=(d, other), device_id_type=MESH)

    def spread_barrier(k):
        for other in digits[k]:
            pl.semaphore_signal(met.at[k], 1, device_id=(d, other), device_id_type=MESH)
        pl.semaphore_wait(met.at[k], len(digits[k]))

    loads = [
        (gp.at[lo, cols(up)], mid.at[0]),
        (gp.at[hi, cols(dn)], mid.at[1]),
        (gp.at[:, cols(d)], own),
        (sm, smv),
        (lr, lv),
        (rr, rv),
        (pr, prv),
    ]
    loads = [pltpu.make_async_copy(a, b, load_sem.at[i]) for i, (a, b) in enumerate(loads)]
    for load in loads:
        load.start()

    pl.semaphore_wait(barrier, 2 + len(sum(digits, [])))

    def rs(p, kind):
        src, dst, to = {
            "a": (gp.at[lo, cols(op), p], far.at[p, 0], up),
            "b": (gp.at[hi, cols(op), p], far.at[p, 1], dn),
            "c": (gp.at[hi, cols(up), p], near.at[p, 1], up),
            "d": (gp.at[lo, cols(dn), p], near.at[p, 2], dn),
            "e": (comb.at[p, 0], near.at[p, 0], up),
            "f": (comb.at[p, 1], near.at[p, 3], dn),
        }[kind]
        n = "abcdef".index(kind)
        return pltpu.make_async_remote_copy(
            src, dst, rs_send.at[p, n], rs_recv.at[p, n], device_id=(to, me), device_id_type=MESH
        )

    def start(p, kinds):
        if p < pieces:
            for kind in kinds:
                rs(p, kind).start()

    def combine(p):
        for h, kind in enumerate("ab"):
            rs(p, kind).wait_recv()

            def add(r, carry, h=h):
                s = mid[h, r, :, p].astype(F32) + far[p, h, r].astype(F32)
                comb[p, h, r] = s.astype(BF16)
                return carry

            lax.fori_loop(0, hb, add, 0)
            rs(p, "ef"[h]).start()

    def exchange(src, dst, p, first, count, send, recv):
        which = pl.ds(first, count)

        def act(t):
            pltpu.make_async_remote_copy(
                src.at[p, t, which], dst.at[p, me, which], send, recv, device_id=(d, t), device_id_type=MESH
            ).start()

        for_peers(act)
        pltpu.make_async_copy(src.at[p, me, which], dst.at[p, me, which], recv).start()

    def fill(m, carry):
        r = lax.broadcasted_iota(jnp.int32, (mrows, wide), 0) + m * mrows
        sel[pl.ds(m * mrows, mrows), :] = jnp.where(r == wide_target, 1.0, 0.0).astype(BF16)
        return carry

    def finish(p):
        for kind in "cdef":
            rs(p, kind).wait_recv()
        for h in range(2):

            def one(r, carry, h=h):
                b = h * hb + r
                g = own[b, :, p].astype(F32) + near[p, h, r].astype(F32)
                gf[b] = g + near[p, 2 + h, r].astype(F32)
                return carry

            lax.fori_loop(0, hb, one, 0)
        blocks = gf[...].reshape(wide, LANES).astype(BF16)

        def pick(m, carry):
            got = jnp.dot(sel[pl.ds(m * mrows, mrows), :], blocks, preferred_element_type=F32)
            outgoing[p, pl.ds(m * 8, 8)] = got.reshape(8, slots, rdev, LANES).astype(BF16)
            return carry

        lax.fori_loop(0, shards // 8, pick, 0)
        if p < last:
            exchange(outgoing, incoming, p, 0, slots, in_send.at[p], in_recv.at[p])
        else:
            for k in range(slots):
                exchange(outgoing, incoming, p, k, 1, in_send.at[p], in_recv.at[p + k])

        def norms(b, carry):
            g = gf[b]
            vnew = BETA2 * smv[b, :, p] + (1.0 - BETA2) * g * g
            adam = g / (jnp.sqrt(vnew) + EPS_ADAM)
            acc[b] = adam * adam if p == 0 else acc[b] + adam * adam
            return carry

        lax.fori_loop(0, brows, norms, 0)

    start(0, "abcd")
    start(1, "ab")
    spread_barrier(0)
    table = ow[d].astype(F32)
    b0 = lax.broadcasted_iota(jnp.int32, (nb, nb), 0)
    b1 = lax.broadcasted_iota(jnp.int32, (nb, nb), 1)
    rows = jnp.broadcast_to(table, (nb, nb))
    column = jnp.sum(jnp.where(b0 == b1, rows, 0.0), axis=1, keepdims=True)
    same = jnp.where(rows == column, 1.0, 0.0)
    rank = jnp.sum(jnp.where(b0 < b1, same, 0.0), axis=0, keepdims=True)
    target = table * float(slots) + rank
    wide = nb * rdev
    e0 = lax.broadcasted_iota(jnp.int32, (nb, wide), 0) * rdev
    e1 = lax.broadcasted_iota(jnp.int32, (nb, wide), 1)
    spread = jnp.where((e1 >= e0) & (e1 < e0 + rdev), 1.0, 0.0).astype(BF16)
    wide_target = jnp.dot(
        jnp.broadcast_to(target, (8, nb)).astype(BF16), spread, preferred_element_type=F32
    )[0:1]
    l1 = lax.broadcasted_iota(jnp.int32, (1, wide), 1)
    wide_target = wide_target.astype(jnp.int32) * rdev + l1 % rdev
    t0 = lax.broadcasted_iota(jnp.int32, (wide, nb), 0)
    t1 = lax.broadcasted_iota(jnp.int32, (wide, nb), 1) * rdev
    tall = jnp.where((t0 >= t1) & (t0 < t1 + rdev), jnp.broadcast_to(target, (wide, nb)), 0.0)
    s0 = lax.broadcasted_iota(jnp.int32, (wide, 1), 0)
    tall_target = jnp.sum(tall, axis=1, keepdims=True).astype(jnp.int32) * rdev + s0 % rdev
    total_rows = shards * slots * rdev
    mrows = 8 * slots * rdev

    for load in loads[:2]:
        load.wait()
    for p in range(pieces + 1):
        if p < pieces:
            combine(p)
            start(p + 1, "cd")
            start(p + 2, "ab")
        if p == 0:
            spread_barrier(1)
            lax.fori_loop(0, total_rows // mrows, fill, 0)
            for load in loads[2:4]:
                load.wait()
        if p > 0:
            finish(p - 1)

    def sum_z(n):
        for i in range(1, NZ):
            pltpu.make_async_remote_copy(
                nsrc.at[n], nz.at[n, z], n_send.at[n, 0], n_recv.at[n, 0],
                device_id=(d, peer(0, i, 0)), device_id_type=MESH,
            ).start()
        pltpu.make_async_copy(nsrc.at[n], nz.at[n, z], n_recv.at[n, 0]).start()

    def sum_plane(n):
        wait_bytes(nz.at[n], n_recv.at[n, 0])
        nmid[n] = jnp.sum(nz[n], axis=0)
        for i in range(1, NY * NC):
            pltpu.make_async_remote_copy(
                nmid.at[n], npl.at[n, y * NC + c], n_send.at[n, 1], n_recv.at[n, 1],
                device_id=(d, peer(i // NC, 0, i % NC)), device_id_type=MESH,
            ).start()
        pltpu.make_async_copy(nmid.at[n], npl.at[n, y * NC + c], n_recv.at[n, 1]).start()

    def summed(n):
        wait_bytes(npl.at[n], n_recv.at[n, 1])
        return jnp.sum(jnp.sum(npl[n], axis=0), axis=0, keepdims=True)[:, :nb]

    sums = jnp.sum(jnp.sum(acc[...].reshape(nb, rdev, LANES), axis=1), axis=1, keepdims=True)
    n0 = lax.broadcasted_iota(jnp.int32, (nb, LANES), 0)
    n1 = lax.broadcasted_iota(jnp.int32, (nb, LANES), 1)
    spots = jnp.where(n0 == n1, jnp.broadcast_to(sums, (nb, LANES)), 0.0)
    nsrc[0] = jnp.sum(spots.reshape(nb // 8, 8, LANES), axis=0)
    sum_z(0)

    for load in loads[4:]:
        load.wait()

    def multiply(p, k):
        g = incoming[p, :, k].astype(F32).reshape(bsize, LANES).astype(BF16)
        got = jnp.dot(lv[k], g, preferred_element_type=F32)
        half[k, :, p * LANES : (p + 1) * LANES] = got.astype(BF16)

    for p in range(last):
        wait_bytes(incoming.at[p], in_recv.at[p])
        for k in range(slots):
            multiply(p, k)
    cut = last * LANES
    for k in range(slots):
        prec[k] = jnp.dot(half[k, :, :cut], rv[k, :cut, :], preferred_element_type=F32)

    def step(p, k):
        x = prec[k, :, p * LANES : (p + 1) * LANES]
        steps[p, :, k] = x.reshape(shards, rdev, LANES).astype(BF16)

    def send_back(p, first, count):
        exchange(steps, returned, p, first, count, ret_send.at[p], ret_recv.at[p])

    early = min(2, pieces)
    pnorms = jnp.zeros((1, nb), F32)
    for k in range(slots):
        wait_bytes(incoming.at[last, :, k], in_recv.at[last + k])
        multiply(last, k)
        total = jnp.zeros((1, bsize), F32)
        for r in range(0, bsize, LANES):
            x = prec[k, r : r + LANES] + jnp.dot(
                half[k, r : r + LANES, cut:], rv[k, cut:, :], preferred_element_type=F32
            )
            prec[k, r : r + LANES] = x
            total += jnp.sum(x * x, axis=0, keepdims=True)
        here = (me * slots + k).astype(F32)
        pnorms += jnp.where(target == here, jnp.sum(total, axis=1, keepdims=True), 0.0)
        if k == 0:
            for p in range(early):
                step(p, k)
                send_back(p, 0, 1)
    nsrc[1] = jnp.zeros((8, LANES), F32)
    nsrc[1, 0:1, :nb] = pnorms
    sum_z(1)
    for p in range(pieces):
        for k in range(1 if p < early else 0, slots):
            step(p, k)
        if p < early:
            send_back(p, 1, slots - 1)
        else:
            send_back(p, 0, slots)
        if p == 0:
            sum_plane(0)
            sum_plane(1)
    for m in range(total_rows // 512):
        r = lax.broadcasted_iota(jnp.int32, (wide, 512), 1) + m * 512
        selt[:, m * 512 : (m + 1) * 512] = jnp.where(r == tall_target, 1.0, 0.0).astype(BF16)
    scale = jnp.sqrt(summed(0)) / (jnp.sqrt(summed(1)) + EPS_NORM)
    tall = jnp.where((t0 >= t1) & (t0 < t1 + rdev), jnp.broadcast_to(scale, (wide, nb)), 0.0)
    tall_scale = jnp.sum(tall, axis=1, keepdims=True) * STEP_RATE

    def ag(p, n):
        src, rows, group, to = [
            (mine, lo, d, up),
            (mine, hi, d, dn),
            (mine, hi, d, up),
            (mine, lo, d, dn),
            (out, lo, dn, up),
            (out, hi, up, dn),
        ][n]
        dst = out.at[rows, cols(group), p]
        src = mine.at[p, rows] if src is mine else dst
        return pltpu.make_async_remote_copy(
            src, dst, ag_send.at[p, n], ag_recv.at[p, n], device_id=(to, me), device_id_type=MESH
        )

    def ag_arrived(p, n):
        rows, group = [(lo, dn), (hi, up), (hi, dn), (lo, up), (lo, op), (hi, op)][n]
        wait_bytes(out.at[rows, cols(group), p], ag_recv.at[p, n])

    keep = [
        pltpu.make_async_copy(mine.at[p], out.at[:, cols(d), p], load_sem.at[p]) for p in range(pieces)
    ]

    def forward(p):
        for n in (0, 1):
            ag_arrived(p, n)
            ag(p, 4 + n).start()

    for p in range(pieces):
        wait_bytes(returned.at[p], ret_recv.at[p])
        back = returned[p].astype(F32).reshape(total_rows, LANES).astype(BF16)
        placed = jnp.dot(selt[...], back, preferred_element_type=F32)
        placed = (placed * tall_scale).reshape(brows, bcols, rdev, LANES)
        mine[p] = (prv[:, :, p].astype(F32) - placed).astype(BF16)
        for n in range(4):
            ag(p, n).start()
        keep[p].start()
        if p > 0:
            forward(p - 1)
    forward(pieces - 1)

    for p in range(pieces):
        for n in range(2, 6):
            ag_arrived(p, n)
        keep[p].wait()
        for n in range(6):
            ag(p, n).wait_send()
        for kind in "abcdef":
            rs(p, kind).wait_send()
        wait_bytes(outgoing.at[p, pl.ds(0, shards - 1)], in_send.at[p])
        wait_bytes(steps.at[p, pl.ds(0, shards - 1)], ret_send.at[p])
    for n in range(2):
        wait_bytes(nz.at[n, pl.ds(0, NZ - 1)], n_send.at[n, 0])
        wait_bytes(npl.at[n, pl.ds(0, NY * NC - 1)], n_send.at[n, 1])


def body(grad_partial, second_moment, params, left_roots, right_roots, owners):
    shards = lax.axis_size("shard")
    brows, rdev, ffall = grad_partial.shape[1:]
    slots, bsize = left_roots.shape[2], left_roots.shape[3]
    ffgroup = second_moment.shape[2]
    bcols = ffgroup // bsize
    groups = ffall // ffgroup
    pieces = bsize // LANES
    hb = brows // 2
    wide = brows * bcols * rdev

    def tiles(x):
        n = x.shape[-1]
        x = x.reshape(brows, rdev, n // LANES, LANES).transpose(0, 2, 1, 3)
        return x.reshape(brows, n // bsize, pieces, rdev, LANES)

    hbm = pl.BlockSpec(memory_space=pl.ANY)
    place = pl.BlockSpec(memory_space=pl.ANY)
    vmem = pl.BlockSpec(memory_space=pltpu.VMEM)
    dma = pltpu.SemaphoreType.DMA
    tile = (rdev, LANES)
    out = pl.pallas_call(
        kernel,
        out_shape=pltpu.VMEM((brows, groups * bcols, pieces) + tile, BF16),
        in_specs=[hbm] * 5 + [vmem],
        out_specs=place,
        scratch_shapes=[
            pltpu.VMEM((brows, bcols, pieces) + tile, BF16),
            pltpu.VMEM((2, hb, bcols, pieces) + tile, BF16),
            pltpu.VMEM((pieces, 2, hb, bcols) + tile, BF16),
            pltpu.VMEM((pieces, 2, hb, bcols) + tile, BF16),
            pltpu.VMEM((pieces, 4, hb, bcols) + tile, BF16),
            pltpu.VMEM((brows, bcols, pieces) + tile, F32),
            pltpu.VMEM((brows, bcols, pieces) + tile, BF16),
            pltpu.VMEM((slots, bsize, bsize), BF16),
            pltpu.VMEM((slots, bsize, bsize), BF16),
            pltpu.VMEM((brows, bcols) + tile, F32),
            pltpu.VMEM((brows, bcols) + tile, F32),
            pltpu.VMEM((shards * slots * rdev, wide), BF16),
            pltpu.VMEM((wide, shards * slots * rdev), BF16),
            pltpu.VMEM((pieces, shards, slots) + tile, BF16),
            pltpu.VMEM((pieces, shards, slots) + tile, BF16),
            pltpu.VMEM((slots, bsize, bsize), BF16),
            pltpu.VMEM((slots, bsize, bsize), F32),
            pltpu.VMEM((pieces, shards, slots) + tile, BF16),
            pltpu.VMEM((pieces, shards, slots) + tile, BF16),
            pltpu.VMEM((pieces, brows, bcols) + tile, BF16),
            pltpu.VMEM((2, 8, LANES), F32),
            pltpu.VMEM((2, NZ, 8, LANES), F32),
            pltpu.VMEM((2, 8, LANES), F32),
            pltpu.VMEM((2, NY * NC, 8, LANES), F32),
            dma((7,)),
            dma((pieces, 6)),
            dma((pieces, 6)),
            dma((pieces,)),
            dma((pieces - 1 + slots,)),
            dma((pieces,)),
            dma((pieces,)),
            dma((pieces, 6)),
            dma((pieces, 6)),
            dma((2, 2)),
            dma((2, 2)),
            pltpu.SemaphoreType.REGULAR((2,)),
        ],
        compiler_params=pltpu.CompilerParams(
            collective_id=0, has_side_effects=True, vmem_limit_bytes=59 * 2**20
        ),
    )(
        tiles(grad_partial[0]),
        tiles(second_moment),
        tiles(params),
        left_roots[0, 0],
        right_roots[0, 0],
        owners.transpose(0, 2, 1),
    )
    out = out.reshape(brows, ffall // LANES, rdev, LANES).transpose(0, 2, 1, 3)
    return out.reshape(brows, rdev, ffall)


def solution(mesh):
    return jax.shard_map(
        body,
        mesh=mesh,
        in_specs=(
            P("dp", None, "shard", None),
            P(None, "shard", "dp"),
            P(None, "shard", "dp"),
            P("dp", "shard", None, None, None),
            P("dp", "shard", None, None, None),
            P(),
        ),
        out_specs=P(None, "shard", None),
        check_vma=False,
    )
```

```python
import functools
import jax
import jax.numpy as jnp
from jax import lax
from jax.experimental import pallas as pl
from jax.experimental.pallas import tpu as pltpu
from jax.sharding import PartitionSpec as P

BETA2 = 0.95
EPS_ADAM = 1e-08
EPS_NORM = 1e-06
STEP_RATE = 0.5
NY, NZ, NC = 4, 8, 2
LANES = 128
MESH = pl.DeviceIdType.MESH
F32, BF16 = jnp.float32, jnp.bfloat16


def wait_bytes(ref, sem):
    pltpu.make_async_copy(ref, ref, sem).wait()


def kernel(
    gp, sm, pr, lr, rr, ow, out,
    own, mid, far, comb, near, smv, prv, lv, rv, gf, acc,
    sel, selt, outgoing, incoming, half, prec, steps, returned, mine,
    nsrc, nz, nmid, npl,
    load_sem, rs_send, rs_recv, in_send, in_recv, ret_send, ret_recv,
    ag_send, ag_recv, n_send, n_recv, met,
):
    brows, bcols, pieces = own.shape[0], own.shape[1], own.shape[2]
    hb = brows // 2
    nb = brows * bcols
    shards, slots, rdev = outgoing.shape[1], outgoing.shape[2], outgoing.shape[3]
    bsize = lv.shape[1]
    d = lax.axis_index("dp")
    me = lax.axis_index("shard")
    y, z, c = me // (NZ * NC), (me // NC) % NZ, me % NC
    up, dn, op = (d + 1) % 4, (d + 3) % 4, (d + 2) % 4
    lo, hi = pl.ds(0, hb), pl.ds(hb, hb)
    last = pieces - 1

    def cols(group):
        return pl.ds(group * bcols, bcols)

    def peer(dy, dz, dc):
        return (((y + dy) % NY) * NZ + (z + dz) % NZ) * NC + (c + dc) % NC

    def for_peers(act):
        def outer(i, carry):
            plane = i // (NZ - 1)
            act(peer(plane // NC, 1 + i % (NZ - 1), plane % NC))
            return carry

        def inner(i, carry):
            act(peer(i // NC, 0, i % NC))
            return carry

        lax.fori_loop(0, (NZ - 1) * NY * NC, outer, 0)
        lax.fori_loop(1, NY * NC, inner, 0)

    zh = NZ // 4
    digits = [
        [peer(i, 0, 0) for i in range(1, NY)],
        [(y * NZ + z // 4 * 4 + (z + i) % 4) * NC + c for i in range(1, 4)],
        [
            (y * NZ + (z // 4 + i // NC) % zh * 4 + z % 4) * NC + (c + i % NC) % NC
            for i in range(1, zh * NC)
        ],
    ]
    barrier = pltpu.get_barrier_semaphore()
    for other in (up, dn):
        pl.semaphore_signal(barrier, 1, device_id=(other, me), device_id_type=MESH)
    for other in sum(digits, []):
        pl.semaphore_signal(barrier, 1, device_id=(d, other), device_id_type=MESH)

    def spread_barrier(k):
        for other in digits[k]:
            pl.semaphore_signal(met.at[k], 1, device_id=(d, other), device_id_type=MESH)
        pl.semaphore_wait(met.at[k], len(digits[k]))

    loads = [
        (gp.at[lo, cols(up)], mid.at[0]),
        (gp.at[hi, cols(dn)], mid.at[1]),
        (gp.at[:, cols(d)], own),
        (sm, smv),
        (lr, lv),
        (rr, rv),
        (pr, prv),
    ]
    loads = [pltpu.make_async_copy(a, b, load_sem.at[i]) for i, (a, b) in enumerate(loads)]
    for load in loads:
        load.start()

    pl.semaphore_wait(barrier, 2 + len(sum(digits, [])))

    def rs(p, kind):
        src, dst, to = {
            "a": (gp.at[lo, cols(op), p], far.at[p, 0], up),
            "b": (gp.at[hi, cols(op), p], far.at[p, 1], dn),
            "c": (gp.at[hi, cols(up), p], near.at[p, 1], up),
            "d": (gp.at[lo, cols(dn), p], near.at[p, 2], dn),
            "e": (comb.at[p, 0], near.at[p, 0], up),
            "f": (comb.at[p, 1], near.at[p, 3], dn),
        }[kind]
        n = "abcdef".index(kind)
        return pltpu.make_async_remote_copy(
            src, dst, rs_send.at[p, n], rs_recv.at[p, n], device_id=(to, me), device_id_type=MESH
        )

    def start(p, kinds):
        if p < pieces:
            for kind in kinds:
                rs(p, kind).start()

    def combine(p):
        for h, kind in enumerate("ab"):
            rs(p, kind).wait_recv()

            def add(r, carry, h=h):
                s = mid[h, r, :, p].astype(F32) + far[p, h, r].astype(F32)
                comb[p, h, r] = s.astype(BF16)
                return carry

            lax.fori_loop(0, hb, add, 0)
            rs(p, "ef"[h]).start()

    def exchange(src, dst, p, first, count, send, recv):
        which = pl.ds(first, count)

        def act(t):
            pltpu.make_async_remote_copy(
                src.at[p, t, which], dst.at[p, me, which], send, recv, device_id=(d, t), device_id_type=MESH
            ).start()

        for_peers(act)
        pltpu.make_async_copy(src.at[p, me, which], dst.at[p, me, which], recv).start()

    def fill(m, carry):
        r = lax.broadcasted_iota(jnp.int32, (mrows, wide), 0) + m * mrows
        sel[pl.ds(m * mrows, mrows), :] = jnp.where(r == wide_target, 1.0, 0.0).astype(BF16)
        return carry

    def finish(p):
        for kind in "cdef":
            rs(p, kind).wait_recv()
        for h in range(2):

            def one(r, carry, h=h):
                b = h * hb + r
                g = own[b, :, p].astype(F32) + near[p, h, r].astype(F32)
                gf[b] = g + near[p, 2 + h, r].astype(F32)
                return carry

            lax.fori_loop(0, hb, one, 0)
        blocks = gf[...].reshape(wide, LANES).astype(BF16)

        def pick(m, carry):
            got = jnp.dot(sel[pl.ds(m * mrows, mrows), :], blocks, preferred_element_type=F32)
            outgoing[p, pl.ds(m * 8, 8)] = got.reshape(8, slots, rdev, LANES).astype(BF16)
            return carry

        lax.fori_loop(0, shards // 8, pick, 0)
        if p < last:
            exchange(outgoing, incoming, p, 0, slots, in_send.at[p], in_recv.at[p])
        else:
            for k in range(slots):
                exchange(outgoing, incoming, p, k, 1, in_send.at[p], in_recv.at[p + k])

        def norms(b, carry):
            g = gf[b]
            vnew = BETA2 * smv[b, :, p] + (1.0 - BETA2) * g * g
            adam = g / (jnp.sqrt(vnew) + EPS_ADAM)
            acc[b] = adam * adam if p == 0 else acc[b] + adam * adam
            return carry

        lax.fori_loop(0, brows, norms, 0)

    start(0, "abcd")
    start(1, "ab")
    spread_barrier(0)
    table = ow[d].astype(F32)
    b0 = lax.broadcasted_iota(jnp.int32, (nb, nb), 0)
    b1 = lax.broadcasted_iota(jnp.int32, (nb, nb), 1)
    rows = jnp.broadcast_to(table, (nb, nb))
    column = jnp.sum(jnp.where(b0 == b1, rows, 0.0), axis=1, keepdims=True)
    same = jnp.where(rows == column, 1.0, 0.0)
    rank = jnp.sum(jnp.where(b0 < b1, same, 0.0), axis=0, keepdims=True)
    target = table * float(slots) + rank
    wide = nb * rdev
    e0 = lax.broadcasted_iota(jnp.int32, (nb, wide), 0) * rdev
    e1 = lax.broadcasted_iota(jnp.int32, (nb, wide), 1)
    spread = jnp.where((e1 >= e0) & (e1 < e0 + rdev), 1.0, 0.0).astype(BF16)
    wide_target = jnp.dot(
        jnp.broadcast_to(target, (8, nb)).astype(BF16), spread, preferred_element_type=F32
    )[0:1]
    l1 = lax.broadcasted_iota(jnp.int32, (1, wide), 1)
    wide_target = wide_target.astype(jnp.int32) * rdev + l1 % rdev
    t0 = lax.broadcasted_iota(jnp.int32, (wide, nb), 0)
    t1 = lax.broadcasted_iota(jnp.int32, (wide, nb), 1) * rdev
    tall = jnp.where((t0 >= t1) & (t0 < t1 + rdev), jnp.broadcast_to(target, (wide, nb)), 0.0)
    s0 = lax.broadcasted_iota(jnp.int32, (wide, 1), 0)
    tall_target = jnp.sum(tall, axis=1, keepdims=True).astype(jnp.int32) * rdev + s0 % rdev
    total_rows = shards * slots * rdev
    mrows = 8 * slots * rdev

    for load in loads[:2]:
        load.wait()
    for p in range(pieces + 1):
        if p < pieces:
            combine(p)
            start(p + 1, "cd")
            start(p + 2, "ab")
        if p == 0:
            spread_barrier(1)
            lax.fori_loop(0, total_rows // mrows, fill, 0)
            for load in loads[2:4]:
                load.wait()
        if p > 0:
            finish(p - 1)

    def sum_z(n):
        for i in range(1, NZ):
            pltpu.make_async_remote_copy(
                nsrc.at[n], nz.at[n, z], n_send.at[n, 0], n_recv.at[n, 0],
                device_id=(d, peer(0, i, 0)), device_id_type=MESH,
            ).start()
        pltpu.make_async_copy(nsrc.at[n], nz.at[n, z], n_recv.at[n, 0]).start()

    def sum_plane(n):
        wait_bytes(nz.at[n], n_recv.at[n, 0])
        nmid[n] = jnp.sum(nz[n], axis=0)
        for i in range(1, NY * NC):
            pltpu.make_async_remote_copy(
                nmid.at[n], npl.at[n, y * NC + c], n_send.at[n, 1], n_recv.at[n, 1],
                device_id=(d, peer(i // NC, 0, i % NC)), device_id_type=MESH,
            ).start()
        pltpu.make_async_copy(nmid.at[n], npl.at[n, y * NC + c], n_recv.at[n, 1]).start()

    def summed(n):
        wait_bytes(npl.at[n], n_recv.at[n, 1])
        return jnp.sum(jnp.sum(npl[n], axis=0), axis=0, keepdims=True)[:, :nb]

    sums = jnp.sum(jnp.sum(acc[...].reshape(nb, rdev, LANES), axis=1), axis=1, keepdims=True)
    n0 = lax.broadcasted_iota(jnp.int32, (nb, LANES), 0)
    n1 = lax.broadcasted_iota(jnp.int32, (nb, LANES), 1)
    spots = jnp.where(n0 == n1, jnp.broadcast_to(sums, (nb, LANES)), 0.0)
    nsrc[0] = jnp.sum(spots.reshape(nb // 8, 8, LANES), axis=0)
    sum_z(0)

    for load in loads[4:]:
        load.wait()

    def multiply(p, k):
        g = incoming[p, :, k].astype(F32).reshape(bsize, LANES).astype(BF16)
        got = jnp.dot(lv[k], g, preferred_element_type=F32)
        half[k, :, p * LANES : (p + 1) * LANES] = got.astype(BF16)

    for p in range(last):
        wait_bytes(incoming.at[p], in_recv.at[p])
        for k in range(slots):
            multiply(p, k)
    cut = last * LANES
    for k in range(slots):
        prec[k] = jnp.dot(half[k, :, :cut], rv[k, :cut, :], preferred_element_type=F32)

    def step(p, k):
        x = prec[k, :, p * LANES : (p + 1) * LANES]
        steps[p, :, k] = x.reshape(shards, rdev, LANES).astype(BF16)

    def send_back(p, first, count):
        exchange(steps, returned, p, first, count, ret_send.at[p], ret_recv.at[p])

    early = min(2, pieces)
    pnorms = jnp.zeros((1, nb), F32)
    for k in range(slots):
        wait_bytes(incoming.at[last, :, k], in_recv.at[last + k])
        multiply(last, k)
        total = jnp.zeros((1, bsize), F32)
        for r in range(0, bsize, LANES):
            x = prec[k, r : r + LANES] + jnp.dot(
                half[k, r : r + LANES, cut:], rv[k, cut:, :], preferred_element_type=F32
            )
            prec[k, r : r + LANES] = x
            total += jnp.sum(x * x, axis=0, keepdims=True)
        here = (me * slots + k).astype(F32)
        pnorms += jnp.where(target == here, jnp.sum(total, axis=1, keepdims=True), 0.0)
        if k == 0:
            for p in range(early):
                step(p, k)
                send_back(p, 0, 1)
    nsrc[1] = jnp.zeros((8, LANES), F32)
    nsrc[1, 0:1, :nb] = pnorms
    sum_z(1)
    for p in range(pieces):
        for k in range(1 if p < early else 0, slots):
            step(p, k)
        if p < early:
            send_back(p, 1, slots - 1)
        else:
            send_back(p, 0, slots)
        if p == 0:
            sum_plane(0)
            sum_plane(1)
    for m in range(total_rows // 512):
        r = lax.broadcasted_iota(jnp.int32, (wide, 512), 1) + m * 512
        selt[:, m * 512 : (m + 1) * 512] = jnp.where(r == tall_target, 1.0, 0.0).astype(BF16)
    scale = jnp.sqrt(summed(0)) / (jnp.sqrt(summed(1)) + EPS_NORM)
    tall = jnp.where((t0 >= t1) & (t0 < t1 + rdev), jnp.broadcast_to(scale, (wide, nb)), 0.0)
    tall_scale = jnp.sum(tall, axis=1, keepdims=True) * STEP_RATE

    def ag(p, n):
        src, rows, group, to = [
            (mine, lo, d, up),
            (mine, hi, d, dn),
            (mine, hi, d, up),
            (mine, lo, d, dn),
            (out, lo, dn, up),
            (out, hi, up, dn),
        ][n]
        dst = out.at[rows, cols(group), p]
        src = mine.at[p, rows] if src is mine else dst
        return pltpu.make_async_remote_copy(
            src, dst, ag_send.at[p, n], ag_recv.at[p, n], device_id=(to, me), device_id_type=MESH
        )

    def ag_arrived(p, n):
        rows, group = [(lo, dn), (hi, up), (hi, dn), (lo, up), (lo, op), (hi, op)][n]
        wait_bytes(out.at[rows, cols(group), p], ag_recv.at[p, n])

    keep = [
        pltpu.make_async_copy(mine.at[p], out.at[:, cols(d), p], load_sem.at[p]) for p in range(pieces)
    ]

    def forward(p):
        for n in (0, 1):
            ag_arrived(p, n)
            ag(p, 4 + n).start()

    for p in range(pieces):
        wait_bytes(returned.at[p], ret_recv.at[p])
        back = returned[p].astype(F32).reshape(total_rows, LANES).astype(BF16)
        placed = jnp.dot(selt[...], back, preferred_element_type=F32)
        placed = (placed * tall_scale).reshape(brows, bcols, rdev, LANES)
        mine[p] = (prv[:, :, p].astype(F32) - placed).astype(BF16)
        for n in range(4):
            ag(p, n).start()
        keep[p].start()
        forward(p)

    for p in range(pieces):
        for n in range(2, 6):
            ag_arrived(p, n)
        keep[p].wait()
        for n in range(6):
            ag(p, n).wait_send()
        for kind in "abcdef":
            rs(p, kind).wait_send()
        wait_bytes(outgoing.at[p, pl.ds(0, shards - 1)], in_send.at[p])
        wait_bytes(steps.at[p, pl.ds(0, shards - 1)], ret_send.at[p])
    for n in range(2):
        wait_bytes(nz.at[n, pl.ds(0, NZ - 1)], n_send.at[n, 0])
        wait_bytes(npl.at[n, pl.ds(0, NY * NC - 1)], n_send.at[n, 1])


def body(grad_partial, second_moment, params, left_roots, right_roots, owners):
    shards = lax.axis_size("shard")
    brows, rdev, ffall = grad_partial.shape[1:]
    slots, bsize = left_roots.shape[2], left_roots.shape[3]
    ffgroup = second_moment.shape[2]
    bcols = ffgroup // bsize
    groups = ffall // ffgroup
    pieces = bsize // LANES
    hb = brows // 2
    wide = brows * bcols * rdev

    def tiles(x):
        n = x.shape[-1]
        x = x.reshape(brows, rdev, n // LANES, LANES).transpose(0, 2, 1, 3)
        return x.reshape(brows, n // bsize, pieces, rdev, LANES)

    hbm = pl.BlockSpec(memory_space=pl.ANY)
    place = pl.BlockSpec(memory_space=pl.ANY)
    vmem = pl.BlockSpec(memory_space=pltpu.VMEM)
    dma = pltpu.SemaphoreType.DMA
    tile = (rdev, LANES)
    out = pl.pallas_call(
        kernel,
        out_shape=pltpu.VMEM((brows, groups * bcols, pieces) + tile, BF16),
        in_specs=[hbm] * 5 + [vmem],
        out_specs=place,
        scratch_shapes=[
            pltpu.VMEM((brows, bcols, pieces) + tile, BF16),
            pltpu.VMEM((2, hb, bcols, pieces) + tile, BF16),
            pltpu.VMEM((pieces, 2, hb, bcols) + tile, BF16),
            pltpu.VMEM((pieces, 2, hb, bcols) + tile, BF16),
            pltpu.VMEM((pieces, 4, hb, bcols) + tile, BF16),
            pltpu.VMEM((brows, bcols, pieces) + tile, F32),
            pltpu.VMEM((brows, bcols, pieces) + tile, BF16),
            pltpu.VMEM((slots, bsize, bsize), BF16),
            pltpu.VMEM((slots, bsize, bsize), BF16),
            pltpu.VMEM((brows, bcols) + tile, F32),
            pltpu.VMEM((brows, bcols) + tile, F32),
            pltpu.VMEM((shards * slots * rdev, wide), BF16),
            pltpu.VMEM((wide, shards * slots * rdev), BF16),
            pltpu.VMEM((pieces, shards, slots) + tile, BF16),
            pltpu.VMEM((pieces, shards, slots) + tile, BF16),
            pltpu.VMEM((slots, bsize, bsize), BF16),
            pltpu.VMEM((slots, bsize, bsize), F32),
            pltpu.VMEM((pieces, shards, slots) + tile, BF16),
            pltpu.VMEM((pieces, shards, slots) + tile, BF16),
            pltpu.VMEM((pieces, brows, bcols) + tile, BF16),
            pltpu.VMEM((2, 8, LANES), F32),
            pltpu.VMEM((2, NZ, 8, LANES), F32),
            pltpu.VMEM((2, 8, LANES), F32),
            pltpu.VMEM((2, NY * NC, 8, LANES), F32),
            dma((7,)),
            dma((pieces, 6)),
            dma((pieces, 6)),
            dma((pieces,)),
            dma((pieces - 1 + slots,)),
            dma((pieces,)),
            dma((pieces,)),
            dma((pieces, 6)),
            dma((pieces, 6)),
            dma((2, 2)),
            dma((2, 2)),
            pltpu.SemaphoreType.REGULAR((2,)),
        ],
        compiler_params=pltpu.CompilerParams(
            collective_id=0, has_side_effects=True, vmem_limit_bytes=59 * 2**20
        ),
    )(
        tiles(grad_partial[0]),
        tiles(second_moment),
        tiles(params),
        left_roots[0, 0],
        right_roots[0, 0],
        owners.transpose(0, 2, 1),
    )
    out = out.reshape(brows, ffall // LANES, rdev, LANES).transpose(0, 2, 1, 3)
    return out.reshape(brows, rdev, ffall)


def solution(mesh):
    return jax.shard_map(
        body,
        mesh=mesh,
        in_specs=(
            P("dp", None, "shard", None),
            P(None, "shard", "dp"),
            P(None, "shard", "dp"),
            P("dp", "shard", None, None, None),
            P("dp", "shard", None, None, None),
            P(),
        ),
        out_specs=P(None, "shard", None),
        check_vma=False,
    )
```

```python
import functools
import jax
import jax.numpy as jnp
from jax import lax
from jax.experimental import pallas as pl
from jax.experimental.pallas import tpu as pltpu
from jax.sharding import PartitionSpec as P

BETA2 = 0.95
EPS_ADAM = 1e-08
EPS_NORM = 1e-06
STEP_RATE = 0.5
NY, NZ, NC = 4, 8, 2
LANES = 128
MESH = pl.DeviceIdType.MESH
F32, BF16 = jnp.float32, jnp.bfloat16


def wait_bytes(ref, sem):
    pltpu.make_async_copy(ref, ref, sem).wait()


def kernel(
    gp, sm, pr, lr, rr, ow, out,
    owv, own, mid, far, comb, near, smv, prv, lv, rv, gf, acc,
    sel, selt, outgoing, incoming, half, prec, steps, returned, mine,
    nsrc, nz, nmid, npl,
    load_sem, rs_send, rs_recv, in_send, in_recv, ret_send, ret_recv,
    ag_send, ag_recv, n_send, n_recv, met,
):
    brows, bcols, pieces = own.shape[0], own.shape[1], own.shape[2]
    hb = brows // 2
    nb = brows * bcols
    shards, slots, rdev = outgoing.shape[1], outgoing.shape[2], outgoing.shape[3]
    bsize = lv.shape[1]
    d = lax.axis_index("dp")
    me = lax.axis_index("shard")
    y, z, c = me // (NZ * NC), (me // NC) % NZ, me % NC
    up, dn, op = (d + 1) % 4, (d + 3) % 4, (d + 2) % 4
    lo, hi = pl.ds(0, hb), pl.ds(hb, hb)
    last = pieces - 1

    def cols(group):
        return pl.ds(group * bcols, bcols)

    def peer(dy, dz, dc):
        return (((y + dy) % NY) * NZ + (z + dz) % NZ) * NC + (c + dc) % NC

    def for_peers(act):
        def outer(i, carry):
            plane = i // (NZ - 1)
            act(peer(plane // NC, 1 + i % (NZ - 1), plane % NC))
            return carry

        def inner(i, carry):
            act(peer(i // NC, 0, i % NC))
            return carry

        lax.fori_loop(0, (NZ - 1) * NY * NC, outer, 0)
        lax.fori_loop(1, NY * NC, inner, 0)

    zh = NZ // 4
    digits = [
        [peer(i, 0, 0) for i in range(1, NY)],
        [(y * NZ + z // 4 * 4 + (z + i) % 4) * NC + c for i in range(1, 4)],
        [
            (y * NZ + (z // 4 + i // NC) % zh * 4 + z % 4) * NC + (c + i % NC) % NC
            for i in range(1, zh * NC)
        ],
    ]
    barrier = pltpu.get_barrier_semaphore()
    for other in (up, dn):
        pl.semaphore_signal(barrier, 1, device_id=(other, me), device_id_type=MESH)
    for other in sum(digits, []):
        pl.semaphore_signal(barrier, 1, device_id=(d, other), device_id_type=MESH)

    def spread_barrier(k):
        for other in digits[k]:
            pl.semaphore_signal(met.at[k], 1, device_id=(d, other), device_id_type=MESH)
        pl.semaphore_wait(met.at[k], len(digits[k]))

    loads = [
        (gp.at[lo, cols(up)], mid.at[0]),
        (gp.at[hi, cols(dn)], mid.at[1]),
        (gp.at[:, cols(d)], own),
        (sm, smv),
        (lr, lv),
        (rr, rv),
        (pr, prv),
        (ow, owv),
    ]
    loads = [pltpu.make_async_copy(a, b, load_sem.at[i]) for i, (a, b) in enumerate(loads)]
    for load in loads[-1:] + loads[:-1]:
        load.start()

    pl.semaphore_wait(barrier, 2 + len(sum(digits, [])))

    def rs(p, kind):
        src, dst, to = {
            "a": (gp.at[lo, cols(op), p], far.at[p, 0], up),
            "b": (gp.at[hi, cols(op), p], far.at[p, 1], dn),
            "c": (gp.at[hi, cols(up), p], near.at[p, 1], up),
            "d": (gp.at[lo, cols(dn), p], near.at[p, 2], dn),
            "e": (comb.at[p, 0], near.at[p, 0], up),
            "f": (comb.at[p, 1], near.at[p, 3], dn),
        }[kind]
        n = "abcdef".index(kind)
        return pltpu.make_async_remote_copy(
            src, dst, rs_send.at[p, n], rs_recv.at[p, n], device_id=(to, me), device_id_type=MESH
        )

    def start(p, kinds):
        if p < pieces:
            for kind in kinds:
                rs(p, kind).start()

    def combine(p):
        for h, kind in enumerate("ab"):
            rs(p, kind).wait_recv()

            def add(r, carry, h=h):
                s = mid[h, r, :, p].astype(F32) + far[p, h, r].astype(F32)
                comb[p, h, r] = s.astype(BF16)
                return carry

            lax.fori_loop(0, hb, add, 0)
            rs(p, "ef"[h]).start()

    def exchange(src, dst, p, first, count, send, recv):
        which = pl.ds(first, count)

        def act(t):
            pltpu.make_async_remote_copy(
                src.at[p, t, which], dst.at[p, me, which], send, recv, device_id=(d, t), device_id_type=MESH
            ).start()

        for_peers(act)
        pltpu.make_async_copy(src.at[p, me, which], dst.at[p, me, which], recv).start()

    def fill(m, carry):
        r = lax.broadcasted_iota(jnp.int32, (mrows, wide), 0) + m * mrows
        sel[pl.ds(m * mrows, mrows), :] = jnp.where(r == wide_target, 1.0, 0.0).astype(BF16)
        return carry

    def finish(p):
        for kind in "cdef":
            rs(p, kind).wait_recv()
        for h in range(2):

            def one(r, carry, h=h):
                b = h * hb + r
                g = own[b, :, p].astype(F32) + near[p, h, r].astype(F32)
                gf[b] = g + near[p, 2 + h, r].astype(F32)
                return carry

            lax.fori_loop(0, hb, one, 0)
        blocks = gf[...].reshape(wide, LANES).astype(BF16)

        def pick(m, carry):
            got = jnp.dot(sel[pl.ds(m * mrows, mrows), :], blocks, preferred_element_type=F32)
            outgoing[p, pl.ds(m * 8, 8)] = got.reshape(8, slots, rdev, LANES).astype(BF16)
            return carry

        lax.fori_loop(0, shards // 8, pick, 0)
        if p < last:
            exchange(outgoing, incoming, p, 0, slots, in_send.at[p], in_recv.at[p])
        else:
            exchange(outgoing, incoming, p, 0, 1, in_send.at[p], in_recv.at[p])
            exchange(outgoing, incoming, p, 1, slots - 1, in_send.at[p], in_recv.at[p + 1])

        def norms(b, carry):
            g = gf[b]
            vnew = BETA2 * smv[b, :, p] + (1.0 - BETA2) * g * g
            adam = g / (jnp.sqrt(vnew) + EPS_ADAM)
            acc[b] = adam * adam if p == 0 else acc[b] + adam * adam
            return carry

        lax.fori_loop(0, brows, norms, 0)

    start(0, "abcd")
    start(1, "ab")
    spread_barrier(0)
    loads[-1].wait()
    table = owv[d].astype(F32)
    b0 = lax.broadcasted_iota(jnp.int32, (nb, nb), 0)
    b1 = lax.broadcasted_iota(jnp.int32, (nb, nb), 1)
    rows = jnp.broadcast_to(table, (nb, nb))
    column = jnp.sum(jnp.where(b0 == b1, rows, 0.0), axis=1, keepdims=True)
    same = jnp.where(rows == column, 1.0, 0.0)
    rank = jnp.sum(jnp.where(b0 < b1, same, 0.0), axis=0, keepdims=True)
    target = table * float(slots) + rank
    wide = nb * rdev
    e0 = lax.broadcasted_iota(jnp.int32, (nb, wide), 0) * rdev
    e1 = lax.broadcasted_iota(jnp.int32, (nb, wide), 1)
    spread = jnp.where((e1 >= e0) & (e1 < e0 + rdev), 1.0, 0.0).astype(BF16)
    wide_target = jnp.dot(
        jnp.broadcast_to(target, (8, nb)).astype(BF16), spread, preferred_element_type=F32
    )[0:1]
    l1 = lax.broadcasted_iota(jnp.int32, (1, wide), 1)
    wide_target = wide_target.astype(jnp.int32) * rdev + l1 % rdev
    t0 = lax.broadcasted_iota(jnp.int32, (wide, nb), 0)
    t1 = lax.broadcasted_iota(jnp.int32, (wide, nb), 1) * rdev
    tall = jnp.where((t0 >= t1) & (t0 < t1 + rdev), jnp.broadcast_to(target, (wide, nb)), 0.0)
    s0 = lax.broadcasted_iota(jnp.int32, (wide, 1), 0)
    tall_target = jnp.sum(tall, axis=1, keepdims=True).astype(jnp.int32) * rdev + s0 % rdev
    total_rows = shards * slots * rdev
    mrows = 8 * slots * rdev

    for load in loads[:2]:
        load.wait()
    def multiply(p, k):
        g = incoming[p, :, k].astype(F32).reshape(bsize, LANES).astype(BF16)
        got = jnp.dot(lv[k], g, preferred_element_type=F32)
        half[k, :, p * LANES : (p + 1) * LANES] = got.astype(BF16)

    def multiply_all(p):
        wait_bytes(incoming.at[p], in_recv.at[p])
        for k in range(slots):
            multiply(p, k)

    for p in range(pieces + 1):
        if p < pieces:
            combine(p)
            start(p + 1, "cd")
            start(p + 2, "ab")
        if p == 0:
            spread_barrier(1)
            lax.fori_loop(0, total_rows // mrows, fill, 0)
            for load in loads[2:4]:
                load.wait()
        if p == pieces:
            for load in loads[4:-1]:
                load.wait()
            multiply_all(0)
        if p > 0:
            finish(p - 1)

    def sum_z(n):
        for i in range(1, NZ):
            pltpu.make_async_remote_copy(
                nsrc.at[n], nz.at[n, z], n_send.at[n, 0], n_recv.at[n, 0],
                device_id=(d, peer(0, i, 0)), device_id_type=MESH,
            ).start()
        pltpu.make_async_copy(nsrc.at[n], nz.at[n, z], n_recv.at[n, 0]).start()

    def sum_plane(n):
        wait_bytes(nz.at[n], n_recv.at[n, 0])
        nmid[n] = jnp.sum(nz[n], axis=0)
        for i in range(1, NY * NC):
            pltpu.make_async_remote_copy(
                nmid.at[n], npl.at[n, y * NC + c], n_send.at[n, 1], n_recv.at[n, 1],
                device_id=(d, peer(i // NC, 0, i % NC)), device_id_type=MESH,
            ).start()
        pltpu.make_async_copy(nmid.at[n], npl.at[n, y * NC + c], n_recv.at[n, 1]).start()

    def summed(n):
        wait_bytes(npl.at[n], n_recv.at[n, 1])
        return jnp.sum(jnp.sum(npl[n], axis=0), axis=0, keepdims=True)[:, :nb]

    sums = jnp.sum(jnp.sum(acc[...].reshape(nb, rdev, LANES), axis=1), axis=1, keepdims=True)
    n0 = lax.broadcasted_iota(jnp.int32, (nb, LANES), 0)
    n1 = lax.broadcasted_iota(jnp.int32, (nb, LANES), 1)
    spots = jnp.where(n0 == n1, jnp.broadcast_to(sums, (nb, LANES)), 0.0)
    nsrc[0] = jnp.sum(spots.reshape(nb // 8, 8, LANES), axis=0)
    sum_z(0)

    for p in range(1, last):
        multiply_all(p)
    cut = last * LANES
    for k in range(slots):
        prec[k] = jnp.dot(half[k, :, :cut], rv[k, :cut, :], preferred_element_type=F32)

    def step(p, k):
        x = prec[k, :, p * LANES : (p + 1) * LANES]
        steps[p, :, k] = x.reshape(shards, rdev, LANES).astype(BF16)

    def send_back(p, first, count):
        exchange(steps, returned, p, first, count, ret_send.at[p], ret_recv.at[p])

    early = min(2, pieces)
    pnorms = jnp.zeros((1, nb), F32)
    for k in range(slots):
        if k == 0:
            wait_bytes(incoming.at[last, :, 0], in_recv.at[last])
        if k == 1:
            wait_bytes(incoming.at[last, :, pl.ds(1, slots - 1)], in_recv.at[last + 1])
        multiply(last, k)
        total = jnp.zeros((1, bsize), F32)
        for r in range(0, bsize, LANES):
            x = prec[k, r : r + LANES] + jnp.dot(
                half[k, r : r + LANES, cut:], rv[k, cut:, :], preferred_element_type=F32
            )
            prec[k, r : r + LANES] = x
            total += jnp.sum(x * x, axis=0, keepdims=True)
        here = (me * slots + k).astype(F32)
        pnorms += jnp.where(target == here, jnp.sum(total, axis=1, keepdims=True), 0.0)
        if k == 0:
            for p in range(early):
                step(p, k)
                send_back(p, 0, 1)
    nsrc[1] = jnp.zeros((8, LANES), F32)
    nsrc[1, 0:1, :nb] = pnorms
    sum_z(1)
    for p in range(pieces):
        for k in range(1 if p < early else 0, slots):
            step(p, k)
        if p < early:
            send_back(p, 1, slots - 1)
        else:
            send_back(p, 0, slots)
        if p == 0:
            sum_plane(0)
            sum_plane(1)
    for m in range(total_rows // 512):
        r = lax.broadcasted_iota(jnp.int32, (wide, 512), 1) + m * 512
        selt[:, m * 512 : (m + 1) * 512] = jnp.where(r == tall_target, 1.0, 0.0).astype(BF16)
    scale = jnp.sqrt(summed(0)) / (jnp.sqrt(summed(1)) + EPS_NORM)
    tall = jnp.where((t0 >= t1) & (t0 < t1 + rdev), jnp.broadcast_to(scale, (wide, nb)), 0.0)
    tall_scale = jnp.sum(tall, axis=1, keepdims=True) * STEP_RATE

    def ag(p, n):
        src, rows, group, to = [
            (mine, lo, d, up),
            (mine, hi, d, dn),
            (mine, hi, d, up),
            (mine, lo, d, dn),
            (out, lo, dn, up),
            (out, hi, up, dn),
        ][n]
        dst = out.at[rows, cols(group), p]
        src = mine.at[p, rows] if src is mine else dst
        return pltpu.make_async_remote_copy(
            src, dst, ag_send.at[p, n], ag_recv.at[p, n], device_id=(to, me), device_id_type=MESH
        )

    def ag_arrived(p, n):
        rows, group = [(lo, dn), (hi, up), (hi, dn), (lo, up), (lo, op), (hi, op)][n]
        wait_bytes(out.at[rows, cols(group), p], ag_recv.at[p, n])

    keep = [
        pltpu.make_async_copy(mine.at[p], out.at[:, cols(d), p], load_sem.at[p]) for p in range(pieces)
    ]

    def forward(p):
        for n in (0, 1):
            ag_arrived(p, n)
            ag(p, 4 + n).start()

    for p in range(pieces):
        wait_bytes(returned.at[p], ret_recv.at[p])
        back = returned[p].astype(F32).reshape(total_rows, LANES).astype(BF16)
        placed = jnp.dot(selt[...], back, preferred_element_type=F32)
        placed = (placed * tall_scale).reshape(brows, bcols, rdev, LANES)
        mine[p] = (prv[:, :, p].astype(F32) - placed).astype(BF16)
        for n in range(4):
            ag(p, n).start()
        keep[p].start()
        forward(p)

    for p in range(pieces):
        for n in range(2, 6):
            ag_arrived(p, n)
        keep[p].wait()
        for n in range(6):
            ag(p, n).wait_send()
        for kind in "abcdef":
            rs(p, kind).wait_send()
        wait_bytes(outgoing.at[p, pl.ds(0, shards - 1)], in_send.at[p])
        wait_bytes(steps.at[p, pl.ds(0, shards - 1)], ret_send.at[p])
    for n in range(2):
        wait_bytes(nz.at[n, pl.ds(0, NZ - 1)], n_send.at[n, 0])
        wait_bytes(npl.at[n, pl.ds(0, NY * NC - 1)], n_send.at[n, 1])


def body(grad_partial, second_moment, params, left_roots, right_roots, owners):
    shards = lax.axis_size("shard")
    brows, rdev, ffall = grad_partial.shape[1:]
    slots, bsize = left_roots.shape[2], left_roots.shape[3]
    ffgroup = second_moment.shape[2]
    bcols = ffgroup // bsize
    groups = ffall // ffgroup
    pieces = bsize // LANES
    hb = brows // 2
    wide = brows * bcols * rdev

    def tiles(x):
        n = x.shape[-1]
        x = x.reshape(brows, rdev, n // LANES, LANES).transpose(0, 2, 1, 3)
        return x.reshape(brows, n // bsize, pieces, rdev, LANES)

    hbm = pl.BlockSpec(memory_space=pl.ANY)
    place = pl.BlockSpec(memory_space=pl.ANY)
    dma = pltpu.SemaphoreType.DMA
    tile = (rdev, LANES)
    out = pl.pallas_call(
        kernel,
        out_shape=pltpu.VMEM((brows, groups * bcols, pieces) + tile, BF16),
        in_specs=[hbm] * 6,
        out_specs=place,
        scratch_shapes=[
            pltpu.VMEM((groups, 1, brows * bcols), jnp.int32),
            pltpu.VMEM((brows, bcols, pieces) + tile, BF16),
            pltpu.VMEM((2, hb, bcols, pieces) + tile, BF16),
            pltpu.VMEM((pieces, 2, hb, bcols) + tile, BF16),
            pltpu.VMEM((pieces, 2, hb, bcols) + tile, BF16),
            pltpu.VMEM((pieces, 4, hb, bcols) + tile, BF16),
            pltpu.VMEM((brows, bcols, pieces) + tile, F32),
            pltpu.VMEM((brows, bcols, pieces) + tile, BF16),
            pltpu.VMEM((slots, bsize, bsize), BF16),
            pltpu.VMEM((slots, bsize, bsize), BF16),
            pltpu.VMEM((brows, bcols) + tile, F32),
            pltpu.VMEM((brows, bcols) + tile, F32),
            pltpu.VMEM((shards * slots * rdev, wide), BF16),
            pltpu.VMEM((wide, shards * slots * rdev), BF16),
            pltpu.VMEM((pieces, shards, slots) + tile, BF16),
            pltpu.VMEM((pieces, shards, slots) + tile, BF16),
            pltpu.VMEM((slots, bsize, bsize), BF16),
            pltpu.VMEM((slots, bsize, bsize), F32),
            pltpu.VMEM((pieces, shards, slots) + tile, BF16),
            pltpu.VMEM((pieces, shards, slots) + tile, BF16),
            pltpu.VMEM((pieces, brows, bcols) + tile, BF16),
            pltpu.VMEM((2, 8, LANES), F32),
            pltpu.VMEM((2, NZ, 8, LANES), F32),
            pltpu.VMEM((2, 8, LANES), F32),
            pltpu.VMEM((2, NY * NC, 8, LANES), F32),
            dma((8,)),
            dma((pieces, 6)),
            dma((pieces, 6)),
            dma((pieces,)),
            dma((pieces + 1,)),
            dma((pieces,)),
            dma((pieces,)),
            dma((pieces, 6)),
            dma((pieces, 6)),
            dma((2, 2)),
            dma((2, 2)),
            pltpu.SemaphoreType.REGULAR((2,)),
        ],
        compiler_params=pltpu.CompilerParams(
            collective_id=0, has_side_effects=True, vmem_limit_bytes=59 * 2**20
        ),
    )(
        tiles(grad_partial[0]),
        tiles(second_moment),
        tiles(params),
        left_roots[0, 0],
        right_roots[0, 0],
        owners.transpose(0, 2, 1),
    )
    out = out.reshape(brows, ffall // LANES, rdev, LANES).transpose(0, 2, 1, 3)
    return out.reshape(brows, rdev, ffall)


def solution(mesh):
    return jax.shard_map(
        body,
        mesh=mesh,
        in_specs=(
            P("dp", None, "shard", None),
            P(None, "shard", "dp"),
            P(None, "shard", "dp"),
            P("dp", "shard", None, None, None),
            P("dp", "shard", None, None, None),
            P(),
        ),
        out_specs=P(None, "shard", None),
        check_vma=False,
    )
```

```python
import functools
import jax
import jax.numpy as jnp
from jax import lax
from jax.experimental import pallas as pl
from jax.experimental.pallas import tpu as pltpu
from jax.sharding import PartitionSpec as P

BETA2 = 0.95
EPS_ADAM = 1e-08
EPS_NORM = 1e-06
STEP_RATE = 0.5
NY, NZ, NC = 4, 8, 2
LANES = 128
MESH = pl.DeviceIdType.MESH
F32, BF16 = jnp.float32, jnp.bfloat16


def wait_bytes(ref, sem):
    pltpu.make_async_copy(ref, ref, sem).wait()


def kernel(
    gp, sm, pr, lr, rr, ow, out,
    owv, own, mid, far, comb, near, smv, prv, lv, rv, gf, acc,
    sel, selt, outgoing, incoming, half, prec, steps, returned, mine,
    nsrc, nz, nmid, npl,
    load_sem, rs_send, rs_recv, in_send, in_recv, ret_send, ret_recv,
    ag_send, ag_recv, n_send, n_recv, met,
):
    brows, bcols, pieces = own.shape[0], own.shape[1], own.shape[2]
    hb = brows // 2
    qb = hb // 2
    nb = brows * bcols
    shards, slots, rdev = outgoing.shape[1], outgoing.shape[2], outgoing.shape[3]
    bsize = lv.shape[1]
    d = lax.axis_index("dp")
    me = lax.axis_index("shard")
    y, z, c = me // (NZ * NC), (me // NC) % NZ, me % NC
    up, dn, op = (d + 1) % 4, (d + 3) % 4, (d + 2) % 4
    lo, hi = pl.ds(0, hb), pl.ds(hb, hb)
    last = pieces - 1

    def cols(group):
        return pl.ds(group * bcols, bcols)

    def peer(dy, dz, dc):
        return (((y + dy) % NY) * NZ + (z + dz) % NZ) * NC + (c + dc) % NC

    def for_peers(act):
        def outer(i, carry):
            plane = i // (NZ - 1)
            act(peer(plane // NC, 1 + i % (NZ - 1), plane % NC))
            return carry

        def inner(i, carry):
            act(peer(i // NC, 0, i % NC))
            return carry

        lax.fori_loop(0, (NZ - 1) * NY * NC, outer, 0)
        lax.fori_loop(1, NY * NC, inner, 0)

    zh = NZ // 4
    digits = [
        [peer(i, 0, 0) for i in range(1, NY)],
        [(y * NZ + z // 4 * 4 + (z + i) % 4) * NC + c for i in range(1, 4)],
        [
            (y * NZ + (z // 4 + i // NC) % zh * 4 + z % 4) * NC + (c + i % NC) % NC
            for i in range(1, zh * NC)
        ],
    ]
    barrier = pltpu.get_barrier_semaphore()
    for other in (up, dn):
        pl.semaphore_signal(barrier, 1, device_id=(other, me), device_id_type=MESH)
    for other in sum(digits, []):
        pl.semaphore_signal(barrier, 1, device_id=(d, other), device_id_type=MESH)

    def spread_barrier(k):
        for other in digits[k]:
            pl.semaphore_signal(met.at[k], 1, device_id=(d, other), device_id_type=MESH)
        pl.semaphore_wait(met.at[k], len(digits[k]))

    loads = [
        (gp.at[lo, cols(up)], mid.at[0]),
        (gp.at[hi, cols(dn)], mid.at[1]),
        (gp.at[:, cols(d)], own),
        (sm, smv),
        (lr, lv),
        (rr, rv),
        (pr, prv),
        (ow, owv),
    ]
    loads = [pltpu.make_async_copy(a, b, load_sem.at[i]) for i, (a, b) in enumerate(loads)]
    for load in loads[-1:] + loads[:-1]:
        load.start()

    pl.semaphore_wait(barrier, 2 + len(sum(digits, [])))

    def rs(p, kind):
        src, dst, to = {
            "a": (gp.at[pl.ds(0, qb), cols(op), p], far.at[p, 0, pl.ds(0, qb)], up),
            "b": (gp.at[pl.ds(hb, qb), cols(op), p], far.at[p, 1, pl.ds(0, qb)], dn),
            "g": (gp.at[pl.ds(qb, qb), cols(op), p], far.at[p, 0, pl.ds(qb, qb)], up),
            "h": (gp.at[pl.ds(hb + qb, qb), cols(op), p], far.at[p, 1, pl.ds(qb, qb)], dn),
            "c": (gp.at[hi, cols(up), p], near.at[p, 1], up),
            "d": (gp.at[lo, cols(dn), p], near.at[p, 2], dn),
            "e": (comb.at[p, 0, pl.ds(0, qb)], near.at[p, 0, pl.ds(0, qb)], up),
            "f": (comb.at[p, 1, pl.ds(0, qb)], near.at[p, 3, pl.ds(0, qb)], dn),
            "i": (comb.at[p, 0, pl.ds(qb, qb)], near.at[p, 0, pl.ds(qb, qb)], up),
            "j": (comb.at[p, 1, pl.ds(qb, qb)], near.at[p, 3, pl.ds(qb, qb)], dn),
        }[kind]
        n = "abcdefghij".index(kind)
        return pltpu.make_async_remote_copy(
            src, dst, rs_send.at[p, n], rs_recv.at[p, n], device_id=(to, me), device_id_type=MESH
        )

    def start(p, kinds):
        if p < pieces:
            for kind in kinds:
                rs(p, kind).start()

    def combine(p):
        for n, kind in enumerate("abgh"):
            h, first = n % 2, n // 2 * qb
            rs(p, kind).wait_recv()

            def add(r, carry, h=h):
                s = mid[h, r, :, p].astype(F32) + far[p, h, r].astype(F32)
                comb[p, h, r] = s.astype(BF16)
                return carry

            lax.fori_loop(first, first + qb, add, 0)
            rs(p, "efij"[n]).start()

    def exchange(src, dst, p, first, count, send, recv):
        which = pl.ds(first, count)

        def act(t):
            pltpu.make_async_remote_copy(
                src.at[p, t, which], dst.at[p, me, which], send, recv, device_id=(d, t), device_id_type=MESH
            ).start()

        for_peers(act)
        pltpu.make_async_copy(src.at[p, me, which], dst.at[p, me, which], recv).start()

    def fill(m, carry):
        r = lax.broadcasted_iota(jnp.int32, (mrows, wide), 0) + m * mrows
        sel[pl.ds(m * mrows, mrows), :] = jnp.where(r == wide_target, 1.0, 0.0).astype(BF16)
        return carry

    def finish(p):
        for kind in "cdefij":
            rs(p, kind).wait_recv()
        for h in range(2):

            def one(r, carry, h=h):
                b = h * hb + r
                g = own[b, :, p].astype(F32) + near[p, h, r].astype(F32)
                gf[b] = g + near[p, 2 + h, r].astype(F32)
                return carry

            lax.fori_loop(0, hb, one, 0)
        blocks = gf[...].reshape(wide, LANES).astype(BF16)

        def pick(m, carry):
            got = jnp.dot(sel[pl.ds(m * mrows, mrows), :], blocks, preferred_element_type=F32)
            outgoing[p, pl.ds(m * 8, 8)] = got.reshape(8, slots, rdev, LANES).astype(BF16)
            return carry

        lax.fori_loop(0, shards // 8, pick, 0)
        if p < last:
            exchange(outgoing, incoming, p, 0, slots, in_send.at[p], in_recv.at[p])
        else:
            exchange(outgoing, incoming, p, 0, 1, in_send.at[p], in_recv.at[p])
            exchange(outgoing, incoming, p, 1, slots - 1, in_send.at[p], in_recv.at[p + 1])

        def norms(b, carry):
            g = gf[b]
            vnew = BETA2 * smv[b, :, p] + (1.0 - BETA2) * g * g
            adam = g / (jnp.sqrt(vnew) + EPS_ADAM)
            acc[b] = adam * adam if p == 0 else acc[b] + adam * adam
            return carry

        lax.fori_loop(0, brows, norms, 0)

    start(0, "abghcd")
    start(1, "abgh")
    spread_barrier(0)
    loads[-1].wait()
    table = owv[d].astype(F32)
    b0 = lax.broadcasted_iota(jnp.int32, (nb, nb), 0)
    b1 = lax.broadcasted_iota(jnp.int32, (nb, nb), 1)
    rows = jnp.broadcast_to(table, (nb, nb))
    column = jnp.sum(jnp.where(b0 == b1, rows, 0.0), axis=1, keepdims=True)
    same = jnp.where(rows == column, 1.0, 0.0)
    rank = jnp.sum(jnp.where(b0 < b1, same, 0.0), axis=0, keepdims=True)
    target = table * float(slots) + rank
    wide = nb * rdev
    e0 = lax.broadcasted_iota(jnp.int32, (nb, wide), 0) * rdev
    e1 = lax.broadcasted_iota(jnp.int32, (nb, wide), 1)
    spread = jnp.where((e1 >= e0) & (e1 < e0 + rdev), 1.0, 0.0).astype(BF16)
    wide_target = jnp.dot(
        jnp.broadcast_to(target, (8, nb)).astype(BF16), spread, preferred_element_type=F32
    )[0:1]
    l1 = lax.broadcasted_iota(jnp.int32, (1, wide), 1)
    wide_target = wide_target.astype(jnp.int32) * rdev + l1 % rdev
    t0 = lax.broadcasted_iota(jnp.int32, (wide, nb), 0)
    t1 = lax.broadcasted_iota(jnp.int32, (wide, nb), 1) * rdev
    tall = jnp.where((t0 >= t1) & (t0 < t1 + rdev), jnp.broadcast_to(target, (wide, nb)), 0.0)
    s0 = lax.broadcasted_iota(jnp.int32, (wide, 1), 0)
    tall_target = jnp.sum(tall, axis=1, keepdims=True).astype(jnp.int32) * rdev + s0 % rdev
    total_rows = shards * slots * rdev
    mrows = 8 * slots * rdev

    for load in loads[:2]:
        load.wait()
    def multiply(p, k):
        g = incoming[p, :, k].astype(F32).reshape(bsize, LANES).astype(BF16)
        got = jnp.dot(lv[k], g, preferred_element_type=F32)
        half[k, :, p * LANES : (p + 1) * LANES] = got.astype(BF16)

    def multiply_all(p):
        wait_bytes(incoming.at[p], in_recv.at[p])
        for k in range(slots):
            multiply(p, k)

    for p in range(pieces + 1):
        if p < pieces:
            combine(p)
            start(p + 1, "cd")
            start(p + 2, "abgh")
        if p == 0:
            spread_barrier(1)
            lax.fori_loop(0, total_rows // mrows, fill, 0)
            for load in loads[2:4]:
                load.wait()
        if p == pieces:
            for load in loads[4:-1]:
                load.wait()
            multiply_all(0)
        if p > 0:
            finish(p - 1)

    def sum_z(n):
        for i in range(1, NZ):
            pltpu.make_async_remote_copy(
                nsrc.at[n], nz.at[n, z], n_send.at[n, 0], n_recv.at[n, 0],
                device_id=(d, peer(0, i, 0)), device_id_type=MESH,
            ).start()
        pltpu.make_async_copy(nsrc.at[n], nz.at[n, z], n_recv.at[n, 0]).start()

    def sum_plane(n):
        wait_bytes(nz.at[n], n_recv.at[n, 0])
        nmid[n] = jnp.sum(nz[n], axis=0)
        for i in range(1, NY * NC):
            pltpu.make_async_remote_copy(
                nmid.at[n], npl.at[n, y * NC + c], n_send.at[n, 1], n_recv.at[n, 1],
                device_id=(d, peer(i // NC, 0, i % NC)), device_id_type=MESH,
            ).start()
        pltpu.make_async_copy(nmid.at[n], npl.at[n, y * NC + c], n_recv.at[n, 1]).start()

    def summed(n):
        wait_bytes(npl.at[n], n_recv.at[n, 1])
        return jnp.sum(jnp.sum(npl[n], axis=0), axis=0, keepdims=True)[:, :nb]

    sums = jnp.sum(jnp.sum(acc[...].reshape(nb, rdev, LANES), axis=1), axis=1, keepdims=True)
    n0 = lax.broadcasted_iota(jnp.int32, (nb, LANES), 0)
    n1 = lax.broadcasted_iota(jnp.int32, (nb, LANES), 1)
    spots = jnp.where(n0 == n1, jnp.broadcast_to(sums, (nb, LANES)), 0.0)
    nsrc[0] = jnp.sum(spots.reshape(nb // 8, 8, LANES), axis=0)
    sum_z(0)

    for p in range(1, last):
        multiply_all(p)
    cut = last * LANES
    for k in range(slots):
        prec[k] = jnp.dot(half[k, :, :cut], rv[k, :cut, :], preferred_element_type=F32)

    def step(p, k):
        x = prec[k, :, p * LANES : (p + 1) * LANES]
        steps[p, :, k] = x.reshape(shards, rdev, LANES).astype(BF16)

    def send_back(p, first, count):
        exchange(steps, returned, p, first, count, ret_send.at[p], ret_recv.at[p])

    early = min(2, pieces)
    pnorms = jnp.zeros((1, nb), F32)
    for k in range(slots):
        if k == 0:
            wait_bytes(incoming.at[last, :, 0], in_recv.at[last])
        if k == 1:
            wait_bytes(incoming.at[last, :, pl.ds(1, slots - 1)], in_recv.at[last + 1])
        multiply(last, k)
        total = jnp.zeros((1, bsize), F32)
        for r in range(0, bsize, LANES):
            x = prec[k, r : r + LANES] + jnp.dot(
                half[k, r : r + LANES, cut:], rv[k, cut:, :], preferred_element_type=F32
            )
            prec[k, r : r + LANES] = x
            total += jnp.sum(x * x, axis=0, keepdims=True)
        here = (me * slots + k).astype(F32)
        pnorms += jnp.where(target == here, jnp.sum(total, axis=1, keepdims=True), 0.0)
        if k == 0:
            for p in range(early):
                step(p, k)
                send_back(p, 0, 1)
    nsrc[1] = jnp.zeros((8, LANES), F32)
    nsrc[1, 0:1, :nb] = pnorms
    sum_z(1)
    for p in range(pieces):
        for k in range(1 if p < early else 0, slots):
            step(p, k)
        if p < early:
            send_back(p, 1, slots - 1)
        else:
            send_back(p, 0, slots)
        if p == 0:
            sum_plane(0)
            sum_plane(1)
    for m in range(total_rows // 512):
        r = lax.broadcasted_iota(jnp.int32, (wide, 512), 1) + m * 512
        selt[:, m * 512 : (m + 1) * 512] = jnp.where(r == tall_target, 1.0, 0.0).astype(BF16)
    scale = jnp.sqrt(summed(0)) / (jnp.sqrt(summed(1)) + EPS_NORM)
    tall = jnp.where((t0 >= t1) & (t0 < t1 + rdev), jnp.broadcast_to(scale, (wide, nb)), 0.0)
    tall_scale = jnp.sum(tall, axis=1, keepdims=True) * STEP_RATE

    def ag(p, n):
        src, rows, group, to = [
            (mine, lo, d, up),
            (mine, hi, d, dn),
            (mine, hi, d, up),
            (mine, lo, d, dn),
            (out, lo, dn, up),
            (out, hi, up, dn),
        ][n]
        dst = out.at[rows, cols(group), p]
        src = mine.at[p, rows] if src is mine else dst
        return pltpu.make_async_remote_copy(
            src, dst, ag_send.at[p, n], ag_recv.at[p, n], device_id=(to, me), device_id_type=MESH
        )

    def ag_arrived(p, n):
        rows, group = [(lo, dn), (hi, up), (hi, dn), (lo, up), (lo, op), (hi, op)][n]
        wait_bytes(out.at[rows, cols(group), p], ag_recv.at[p, n])

    keep = [
        pltpu.make_async_copy(mine.at[p], out.at[:, cols(d), p], load_sem.at[p]) for p in range(pieces)
    ]

    def forward(p):
        for n in (0, 1):
            ag_arrived(p, n)
            ag(p, 4 + n).start()

    for p in range(pieces):
        wait_bytes(returned.at[p], ret_recv.at[p])
        back = returned[p].astype(F32).reshape(total_rows, LANES).astype(BF16)
        placed = jnp.dot(selt[...], back, preferred_element_type=F32)
        placed = (placed * tall_scale).reshape(brows, bcols, rdev, LANES)
        mine[p] = (prv[:, :, p].astype(F32) - placed).astype(BF16)
        for n in range(4):
            ag(p, n).start()
        keep[p].start()
        forward(p)

    for p in range(pieces):
        for n in range(2, 6):
            ag_arrived(p, n)
        keep[p].wait()
        for n in range(6):
            ag(p, n).wait_send()
        for kind in "abcdefghij":
            rs(p, kind).wait_send()
        wait_bytes(outgoing.at[p, pl.ds(0, shards - 1)], in_send.at[p])
        wait_bytes(steps.at[p, pl.ds(0, shards - 1)], ret_send.at[p])
    for n in range(2):
        wait_bytes(nz.at[n, pl.ds(0, NZ - 1)], n_send.at[n, 0])
        wait_bytes(npl.at[n, pl.ds(0, NY * NC - 1)], n_send.at[n, 1])


def body(grad_partial, second_moment, params, left_roots, right_roots, owners):
    shards = lax.axis_size("shard")
    brows, rdev, ffall = grad_partial.shape[1:]
    slots, bsize = left_roots.shape[2], left_roots.shape[3]
    ffgroup = second_moment.shape[2]
    bcols = ffgroup // bsize
    groups = ffall // ffgroup
    pieces = bsize // LANES
    hb = brows // 2
    wide = brows * bcols * rdev

    def tiles(x):
        n = x.shape[-1]
        x = x.reshape(brows, rdev, n // LANES, LANES).transpose(0, 2, 1, 3)
        return x.reshape(brows, n // bsize, pieces, rdev, LANES)

    hbm = pl.BlockSpec(memory_space=pl.ANY)
    place = pl.BlockSpec(memory_space=pl.ANY)
    dma = pltpu.SemaphoreType.DMA
    tile = (rdev, LANES)
    out = pl.pallas_call(
        kernel,
        out_shape=pltpu.VMEM((brows, groups * bcols, pieces) + tile, BF16),
        in_specs=[hbm] * 6,
        out_specs=place,
        scratch_shapes=[
            pltpu.VMEM((groups, 1, brows * bcols), jnp.int32),
            pltpu.VMEM((brows, bcols, pieces) + tile, BF16),
            pltpu.VMEM((2, hb, bcols, pieces) + tile, BF16),
            pltpu.VMEM((pieces, 2, hb, bcols) + tile, BF16),
            pltpu.VMEM((pieces, 2, hb, bcols) + tile, BF16),
            pltpu.VMEM((pieces, 4, hb, bcols) + tile, BF16),
            pltpu.VMEM((brows, bcols, pieces) + tile, F32),
            pltpu.VMEM((brows, bcols, pieces) + tile, BF16),
            pltpu.VMEM((slots, bsize, bsize), BF16),
            pltpu.VMEM((slots, bsize, bsize), BF16),
            pltpu.VMEM((brows, bcols) + tile, F32),
            pltpu.VMEM((brows, bcols) + tile, F32),
            pltpu.VMEM((shards * slots * rdev, wide), BF16),
            pltpu.VMEM((wide, shards * slots * rdev), BF16),
            pltpu.VMEM((pieces, shards, slots) + tile, BF16),
            pltpu.VMEM((pieces, shards, slots) + tile, BF16),
            pltpu.VMEM((slots, bsize, bsize), BF16),
            pltpu.VMEM((slots, bsize, bsize), F32),
            pltpu.VMEM((pieces, shards, slots) + tile, BF16),
            pltpu.VMEM((pieces, shards, slots) + tile, BF16),
            pltpu.VMEM((pieces, brows, bcols) + tile, BF16),
            pltpu.VMEM((2, 8, LANES), F32),
            pltpu.VMEM((2, NZ, 8, LANES), F32),
            pltpu.VMEM((2, 8, LANES), F32),
            pltpu.VMEM((2, NY * NC, 8, LANES), F32),
            dma((8,)),
            dma((pieces, 10)),
            dma((pieces, 10)),
            dma((pieces,)),
            dma((pieces + 1,)),
            dma((pieces,)),
            dma((pieces,)),
            dma((pieces, 6)),
            dma((pieces, 6)),
            dma((2, 2)),
            dma((2, 2)),
            pltpu.SemaphoreType.REGULAR((2,)),
        ],
        compiler_params=pltpu.CompilerParams(
            collective_id=0, has_side_effects=True, vmem_limit_bytes=59 * 2**20
        ),
    )(
        tiles(grad_partial[0]),
        tiles(second_moment),
        tiles(params),
        left_roots[0, 0],
        right_roots[0, 0],
        owners.transpose(0, 2, 1),
    )
    out = out.reshape(brows, ffall // LANES, rdev, LANES).transpose(0, 2, 1, 3)
    return out.reshape(brows, rdev, ffall)


def solution(mesh):
    return jax.shard_map(
        body,
        mesh=mesh,
        in_specs=(
            P("dp", None, "shard", None),
            P(None, "shard", "dp"),
            P(None, "shard", "dp"),
            P("dp", "shard", None, None, None),
            P("dp", "shard", None, None, None),
            P(),
        ),
        out_specs=P(None, "shard", None),
        check_vma=False,
    )
```
